128 devices in a mesh: pipe: 4 (over y), seq: 32 (over z, x, core).
Axes of the slice: x: 4, y: 4, z: 4, core: 2. Of those that a mesh axis runs over, the one named last changes fastest.
Arguments:
- hidden_in: bfloat16 [3072, 1536], P('seq'), may hold values from -6 to 6
- modulation: float32 [4, 3, 1536], P('pipe'), may hold values from -3 to 3
- w_qkv: bfloat16 [4, 1536, 4608], P('pipe'), may hold values from -0.15625 to 0.15625
- w_out: bfloat16 [4, 1536, 1536], P('pipe'), may hold values from -0.15625 to 0.15625
- qk_gain: float32 [4, 2, 128], P('pipe'), may hold values from 1.2 to 2.4
- stale_kv: bfloat16 [4, 3072, 2, 1536], P('pipe', 'seq'), may hold values from -6 to 6
- positions: int32 [3072, 3], P('seq'), may hold values from 0 to 63, as said below
- order: int32 [4], replicated, may hold values from 0 to 3, each once
Outputs:
- hidden_out: bfloat16 [4, 3072, 1536], P('pipe', 'seq')
- fresh_kv: bfloat16 [4, 3072, 2, 1536], P('pipe', 'seq')
The draws below stay inside these ranges and needn't reach their ends.
Inputs may be any that keep to these rules, and one draw needn't show every extreme that they name: `positions`: distinct tokens have distinct (row, column); the text index is below 4, the row below 48 and the column below 64. `order`: each patch number once.
All inputs are finite; a program needn't handle non-finite values.
Results may differ from the reference program's by a relative error of at most 0.04.
Values may be sent and summed in bfloat16 or wider, within the bound.
No kernel may reach another device: no remote copies, remote signals or barrier semaphores. Data moves between devices by JAX's collectives and lax.ppermute only.
A program may use at most 64 MiB of HBM per device.

```python
import math
import jax
import jax.numpy as jnp
from jax import lax

D = 1536
HEADS = 12
HEAD_DIM = 128
GRID_COLS = 64
PATCHES = 4
TOK_DEV = 96
LAYERS = 4
TOKENS = 3072
PATCH_DEV = 24
PATCH_TOKENS = 768
N_SEQ = 32


def draw_positions(key, part):
    key = jax.random.fold_in(key, 7)
    first_key, second_key = jax.random.split(key)
    placed = jax.random.permutation(first_key, TOKENS).astype(jnp.int32)
    text_index = jax.random.randint(second_key, (TOKENS,), 0, 4, dtype=jnp.int32)
    return jnp.stack([text_index, placed // GRID_COLS, placed % GRID_COLS], axis=1)


def shard_levels(stream_key, shape, cuts, low, high):
    level, own = 1.0, jax.random.fold_in(stream_key, 6)
    for dim, parts in cuts:
        steps = jnp.exp(jax.random.uniform(jax.random.fold_in(own, dim), (parts,), jnp.float32, low / len(cuts), high / len(cuts)))
        level = level * jnp.repeat(steps, shape[dim] // parts).reshape([-1 if axis == dim else 1 for axis in range(len(shape))])
    return level


def normal_values(rng, shape, scale, limit, cuts=(), held_as=jnp.bfloat16):
    factor_of = shard_levels(rng, shape, cuts, -0.22, 0.18) if cuts else 1.0
    values = jax.random.normal(rng, shape, jnp.float32) * scale * factor_of
    return jnp.minimum(jnp.maximum(values, -limit), limit).astype(held_as)


def setup_inputs(seed: int = 0) -> dict:
    key_of = jax.random.split(jax.random.key(seed), 9)
    hidden_in = normal_values(key_of[0], (TOKENS, D), 1.0, 6.0, ((0, 32),))
    modulation = normal_values(key_of[1], (LAYERS, 3, D), 0.5, 3.0, ((0, 4),), jnp.float32)
    w_qkv = normal_values(key_of[2], (LAYERS, D, 3 * HEADS * HEAD_DIM), D ** -0.5, 0.15625, ((0, 4),))
    w_out = normal_values(key_of[3], (LAYERS, HEADS * HEAD_DIM, D), (HEADS * HEAD_DIM) ** -0.5, 0.15625, ((0, 4),))
    qk_gain = jnp.clip(jnp.exp(math.log(2.4) - 0.6931472 * jax.random.uniform(key_of[4], (LAYERS, 2, HEAD_DIM), jnp.float32) ** shard_levels(key_of[4], (LAYERS, 2, HEAD_DIM), ((0, 4),), -0.2, 0.2)), 1.2, 2.4)
    stale_kv = normal_values(key_of[5], (LAYERS, TOKENS, 2, HEADS * HEAD_DIM), 1.0, 6.0, ((0, 4), (1, 32)))
    positions = draw_positions(jax.random.fold_in(key_of[8], 71), 0)
    order = jax.random.permutation(key_of[7], PATCHES).astype(jnp.int32)
    return dict(hidden_in=hidden_in, modulation=modulation, w_qkv=w_qkv, w_out=w_out, qk_gain=qk_gain, stale_kv=stale_kv, positions=positions, order=order)


def rotary_tables(positions):
    pair_index = jnp.arange(64)
    axis_pick = jnp.where(pair_index < 8, 0, jnp.where(pair_index < 36, 1, 2))
    axis_start = jnp.where(pair_index < 8, 0, jnp.where(pair_index < 36, 8, 36))
    axis_width = jnp.where(pair_index < 8, 16.0, 56.0).astype(jnp.float32)
    inner_index = (pair_index - axis_start).astype(jnp.float32)
    frequency = jnp.power(jnp.float32(10000.0), -2.0 * inner_index / axis_width)
    one_hot = (jnp.arange(3)[:, None] == axis_pick[None, :]).astype(jnp.float32)
    coords = positions.astype(jnp.float32)
    picked = lax.optimization_barrier(jnp.sum(coords[:, :, None] * one_hot[None, :, :], axis=1))
    angles = picked * frequency[None, :]
    return (jnp.cos(angles), jnp.sin(angles))

def rotate(heads_in, cosine, sine_part):
    shaped = heads_in.reshape(heads_in.shape[0], heads_in.shape[1], 64, 2)
    even_part = shaped[..., 0]
    odd_part = shaped[..., 1]
    cos_rows = cosine[:, None, :]
    sin_rows = sine_part[:, None, :]
    turned = jnp.stack([cos_rows * even_part - sin_rows * odd_part, sin_rows * even_part + cos_rows * odd_part], axis=-1)
    return turned.reshape(heads_in.shape)

def head_norm(heads_in, gain_row):
    return heads_in * (1.0 / jnp.sqrt(lax.optimization_barrier(jnp.mean(heads_in * heads_in, axis=-1, keepdims=True)) + 1e-06)) * gain_row

def modulate(hidden, shift_row, scale_row):
    values = hidden.astype(jnp.float32)
    centred = values - lax.optimization_barrier(jnp.mean(values, axis=-1, keepdims=True))
    spread = lax.optimization_barrier(jnp.mean(centred * centred, axis=-1, keepdims=True))
    return (centred / jnp.sqrt(spread + 1e-06) * (1.0 + scale_row) + shift_row).astype(jnp.bfloat16)

def reference(hidden_in, modulation, w_qkv, w_out, qk_gain, stale_kv, positions, order):
    width_heads = HEADS * HEAD_DIM
    scale_factor = 1.0 / math.sqrt(HEAD_DIM)
    cos_all, sin_all = rotary_tables(positions)
    token_patch = jnp.arange(TOKENS) // PATCH_DEV % PATCHES
    patch_rank = jnp.zeros((PATCHES,), jnp.int32).at[order].set(jnp.arange(PATCHES, dtype=jnp.int32))
    token_rank = patch_rank[token_patch]
    within = jnp.arange(PATCH_TOKENS)
    base_rows = within // PATCH_DEV * TOK_DEV + within % PATCH_DEV
    hidden = hidden_in
    layer_outs = []
    fresh_list = []
    for layer_index in range(LAYERS):
        shift_row = modulation[layer_index, 0]
        scale_row = modulation[layer_index, 1]
        gate_row = modulation[layer_index, 2]
        modulated = modulate(hidden, shift_row, scale_row)
        projected = jnp.dot(modulated, w_qkv[layer_index], preferred_element_type=jnp.float32)
        query_raw = projected[:, :width_heads].reshape(TOKENS, HEADS, HEAD_DIM)
        fresh_pair = jnp.stack([projected[:, width_heads:2 * width_heads], projected[:, 2 * width_heads:]], axis=1).astype(jnp.bfloat16)
        queries = rotate(head_norm(query_raw, qk_gain[layer_index, 0]), cos_all, sin_all).astype(jnp.bfloat16)
        updated = hidden
        for rank_index in range(PATCHES):
            patch_id = order[rank_index]
            row_ids = base_rows + patch_id * PATCH_DEV
            use_fresh = (token_rank <= rank_index)[:, None, None]
            buffer = jnp.where(use_fresh, fresh_pair, stale_kv[layer_index])
            key_raw = buffer[:, 0].astype(jnp.float32).reshape(TOKENS, HEADS, HEAD_DIM)
            key_hats = rotate(head_norm(key_raw, qk_gain[layer_index, 1]), cos_all, sin_all).astype(jnp.bfloat16)
            values = buffer[:, 1].reshape(TOKENS, HEADS, HEAD_DIM)
            query_rows = queries[row_ids].astype(jnp.float32)
            scores = jnp.einsum('qhd,khd->hqk', query_rows, key_hats.astype(jnp.float32)) * scale_factor
            weights = jnp.exp(scores)
            denominator = lax.optimization_barrier(jnp.sum(weights, axis=2))
            rounded = lax.optimization_barrier(weights.astype(jnp.bfloat16)).astype(jnp.float32)
            rounded = rounded.reshape(HEADS, PATCH_TOKENS, N_SEQ, TOK_DEV)
            blocks = jnp.einsum('hqnk,nkhd->nqhd', rounded, values.astype(jnp.float32).reshape(N_SEQ, TOK_DEV, HEADS, HEAD_DIM))
            blocks = lax.optimization_barrier(blocks.astype(jnp.bfloat16)).astype(jnp.float32)
            numerator = lax.optimization_barrier(jnp.sum(blocks, axis=0))
            attended = (numerator / jnp.transpose(denominator)[:, :, None]).astype(jnp.bfloat16).reshape(PATCH_TOKENS, width_heads)
            branch_out = jnp.dot(attended, w_out[layer_index], preferred_element_type=jnp.float32)
            new_rows = (hidden[row_ids].astype(jnp.float32) + gate_row * branch_out).astype(jnp.bfloat16)
            updated = updated.at[row_ids].set(new_rows)
        layer_outs.append(updated)
        fresh_list.append(fresh_pair)
        hidden = updated
    return (jnp.stack(layer_outs), jnp.stack(fresh_list))
```

```python
import functools
import math

import jax
import jax.numpy as jnp
import numpy as np
from jax import lax
from jax.experimental import pallas as pl
from jax.experimental.pallas import tpu as pltpu
from jax.sharding import Mesh
from jax.sharding import PartitionSpec as P

GROUPS = 2
PATCHES = 4
HEAD = 128
HEADS = 12
CHIPS = 16
PD = 24
D = 1536
LAYERS = 4
PER = PATCHES // GROUPS
N = PER * PD
KEYS = 2 * CHIPS * PD
F32 = jnp.float32
BF16 = jnp.bfloat16


def rotary_tables(positions):
    lane = np.arange(HEAD)
    pair = lane // 2
    axis = np.where(pair < 8, 0, np.where(pair < 36, 1, 2))
    start = np.where(pair < 8, 0, np.where(pair < 36, 8, 36))
    width = np.where(pair < 8, 16.0, 56.0)
    freq = jnp.asarray(np.power(10000.0, -2.0 * (pair - start) / width).astype(np.float32))[None]
    c = positions.astype(F32)
    picked = jnp.where(axis[None] == 0, c[:, 0:1], jnp.where(axis[None] == 1, c[:, 1:2], c[:, 2:3]))
    angle = picked * freq
    cos, sin = jnp.cos(angle), jnp.sin(angle)
    even = (lane % 2 == 0)[None]
    down = jnp.where(even, -sin, 0.0)
    up = jnp.where(even, 0.0, sin)
    return jnp.concatenate([cos, down, up], axis=1).reshape(PATCHES, PD, 3 * HEAD)


def hats(x, gain, tab):
    inv = lax.rsqrt(jnp.mean(x * x, axis=-1, keepdims=True) + 1e-6)
    x = x * inv * gain
    return (
        x * tab[:, :HEAD]
        + pltpu.roll(x, HEAD - 1, 1) * tab[:, HEAD : 2 * HEAD]
        + pltpu.roll(x, 1, 1) * tab[:, 2 * HEAD :]
    )


def stage(info_ref, turn):
    section = info_ref[0]
    g = jnp.clip(turn - section, 0, GROUPS - 1)
    ids = [info_ref[1 + g * PER + j] for j in range(PER)]
    return section, g, ids


def rows_of(info_ref, turn, x_ref, recv_ref):
    section, _, ids = stage(info_ref, turn)
    own = jnp.concatenate([x_ref[p].astype(F32) for p in ids], axis=0)
    if recv_ref is None:
        return own
    return jnp.where(section == 0, own, recv_ref[...].astype(F32))


def project_kernel(turn, *refs):
    first = turn == 0
    refs = list(refs)
    info_ref, x_ref = refs[:2]
    refs = refs[2:]
    recv_ref = None if first else refs.pop(0)
    mod_ref, w_ref, gain_ref, tab_ref = refs[:4]
    refs = refs[4:]
    stale_ref = refs.pop(0) if first else None
    chunk_ref, fresh_ref = refs
    _, _, ids = stage(info_ref, turn)
    rows = rows_of(info_ref, turn, x_ref, recv_ref)
    centred = rows - jnp.mean(rows, axis=-1, keepdims=True)
    spread = jnp.mean(centred * centred, axis=-1, keepdims=True)
    modulated = (
        centred * lax.rsqrt(spread + 1e-6) * (1.0 + mod_ref[0, 1:2, :]) + mod_ref[0, 0:1, :]
    ).astype(BF16)
    q_gain = gain_ref[0, 0:1, :] * (math.log2(math.e) / math.sqrt(HEAD))
    k_gain = gain_ref[0, 1:2, :]
    tab = jnp.concatenate([tab_ref[p] for p in ids], axis=0)
    wide = 4 * HEAD
    for block in range(D // wide):
        q, k, v = (
            jnp.dot(
                modulated,
                w_ref[0, :, part * D + block * wide : part * D + (block + 1) * wide],
                preferred_element_type=F32,
            )
            for part in range(3)
        )
        k16, v16 = k.astype(BF16), v.astype(BF16)
        fresh_ref[:, block * wide : (block + 1) * wide] = k16
        fresh_ref[:, D + block * wide : D + (block + 1) * wide] = v16
        k, v = k16.astype(F32), v16.astype(F32)
        for i in range(wide // HEAD):
            h = block * (wide // HEAD) + i
            lanes = slice(i * HEAD, (i + 1) * HEAD)
            qh = hats(q[:, lanes], q_gain, tab)
            kh = hats(k[:, lanes], k_gain, tab)
            vh = v[:, lanes]
            parts = []
            for j in range(PER):
                here = slice(PD * j, PD * (j + 1))
                parts += [qh[here], kh[here], vh[here]]
            if first:
                for r in range(1, PATCHES):
                    p = info_ref[1 + r]
                    ks = stale_ref[p, :, h * HEAD : (h + 1) * HEAD].astype(F32)
                    vs = stale_ref[p, :, D + h * HEAD : D + (h + 1) * HEAD].astype(F32)
                    parts += [hats(ks, k_gain, tab_ref[p]), vs]
            chunk_ref[h] = jnp.concatenate(parts, axis=0).astype(BF16)
    for c in range(HEADS, CHIPS):
        chunk_ref[c] = jnp.zeros(chunk_ref.shape[1:], BF16)


def attend_kernel(turn, last, *refs):
    first = turn == 0
    refs = list(refs)
    info_ref, own_ref, oth_ref = refs[:3]
    refs = refs[3:]
    kin_ref, vin_ref = (None, None) if first else (refs.pop(0), refs.pop(0))
    out_ref = refs.pop(0)
    kout_ref, vout_ref = (None, None) if last else (refs.pop(0), refs.pop(0))
    kown_ref, vown_ref = refs
    section, g, _ = stage(info_ref, turn)
    own = own_ref[...].astype(F32)
    oth = oth_ref[...].astype(F32)

    def pick(x, start):
        return x[:, start : start + PD, :].reshape(CHIPS * PD, HEAD)

    def both(start):
        return jnp.concatenate([pick(own, start), pick(oth, start)], axis=0).astype(BF16)

    if first:
        kin_ref, vin_ref = kout_ref, vout_ref
        for r in range(1, PATCHES):
            start = PER * 3 * PD + (r - 1) * 2 * PD
            kin_ref[r] = both(start)
            vin_ref[r] = both(start + PD)
        base = 0
    else:
        base = g * PER
    ones = jnp.ones((KEYS, HEAD), BF16)
    outs = []
    for j in range(PER):
        kown_ref[j] = both(3 * PD * j + PD)
        vown_ref[j] = both(3 * PD * j + 2 * PD)
        q = pick(own, 3 * PD * j).astype(BF16)
        total = jnp.zeros((CHIPS * PD, 2 * HEAD), F32)
        for i in range(PATCHES):
            if i <= j:
                k, v = kown_ref[i], vown_ref[i]
            else:
                n = i - j - 1
                slot = n + j + 1 if first else jnp.where(n < base, n, n + j + 1)
                k, v = kin_ref[slot], vin_ref[slot]
            s = lax.dot_general(q, k, (((1,), (1,)), ((), ())), preferred_element_type=F32)
            w = jnp.exp2(s).astype(BF16)
            total = total + jnp.dot(
                w, jnp.concatenate([v, ones], axis=1), preferred_element_type=F32
            )
        att = total[:, :HEAD] / total[:, HEAD:]
        outs.append(att.reshape(CHIPS, PD, HEAD))
    out_ref[...] = jnp.concatenate(outs, axis=1).astype(BF16)
    if last:
        return
    begun = turn >= section
    if not first:
        for n in range(PATCHES - PER):
            slot = jnp.where(n < base, n, n + PER)
            kout_ref[slot] = kin_ref[slot]
            vout_ref[slot] = vin_ref[slot]
    elif PER < PATCHES:
        kin_ref[0] = kown_ref[0]
        vin_ref[0] = vown_ref[0]
    for j in range(PER):
        kout_ref[base + j] = jnp.where(begun, kown_ref[j], kin_ref[base + j])
        vout_ref[base + j] = jnp.where(begun, vown_ref[j], vin_ref[base + j])


def output_kernel(turn, last, *refs):
    first = turn == 0
    refs = list(refs)
    info_ref, att_ref, w_ref, x_ref = refs[:4]
    refs = refs[4:]
    recv_ref = None if first else refs.pop(0)
    mod_ref = refs.pop(0)
    att = jnp.concatenate([att_ref[h] for h in range(HEADS)], axis=1)
    rows = rows_of(info_ref, turn, x_ref, recv_ref)
    branch = jnp.dot(att, w_ref[0], preferred_element_type=F32)
    new = rows + mod_ref[0, 2:3, :] * branch
    if not last:
        refs[0][...] = new.astype(BF16)
        return
    *olds, out_ref = refs
    for section in range(LAYERS):

        @pl.when(info_ref[0] == section)
        def _():
            for g in range(GROUPS):
                rows = new if section + g == turn else olds[section + g][...].astype(F32)
                for j in range(PER):
                    p = info_ref[1 + g * PER + j]
                    out_ref[p] = rows[PD * j : PD * (j + 1)].astype(BF16)


def collect_kernel(info_ref, *refs):
    *olds, out_ref = refs
    for section in range(LAYERS):

        @pl.when(info_ref[0] == section)
        def _():
            for g in range(GROUPS):
                rows = olds[section + g][...].astype(F32)
                for j in range(PER):
                    p = info_ref[1 + g * PER + j]
                    out_ref[p] = rows[PD * j : PD * (j + 1)].astype(BF16)


SMEM = pl.BlockSpec(memory_space=pltpu.SMEM)
VMEM = pl.BlockSpec(memory_space=pltpu.VMEM)


def shape(*dims, dtype=BF16):
    return jax.ShapeDtypeStruct(dims, dtype)


def call(kernel, name, out_shape, args, limit, scratch=()):
    return pl.pallas_call(
        kernel,
        out_shape=out_shape,
        in_specs=[SMEM] + [VMEM] * (len(args) - 1),
        out_specs=[VMEM] * len(out_shape),
        scratch_shapes=list(scratch),
        compiler_params=pltpu.CompilerParams(vmem_limit_bytes=limit * 2**20),
        name=name,
    )(*args)


def on_device(hidden_in, modulation, w_qkv, w_out, qk_gain, stale_kv, positions, order):
    section = lax.axis_index("pipe")
    info = jnp.concatenate([jnp.stack([section]).astype(jnp.int32), order])
    x = hidden_in.reshape(PATCHES, PD, D)
    stale = stale_kv[0].reshape(PATCHES, PD, 2 * D)
    tab = rotary_tables(positions)
    turns = GROUPS + LAYERS - 1
    recv = kbuf = vbuf = None
    fresh, hidden = [], []
    for turn in range(turns):
        first, last = turn == 0, turn == turns - 1
        rows = PER * 3 * PD + (3 * 2 * PD if first else 0)
        args = [info, x] + ([] if first else [recv]) + [modulation, w_qkv, qk_gain, tab]
        args += [stale] if first else []
        chunk, raw = call(
            functools.partial(project_kernel, turn),
            f"project{turn}",
            [shape(CHIPS, rows, HEAD), shape(N, 2 * D)],
            args,
            20,
        )
        fresh.append(raw)
        own = lax.all_to_all(chunk, ("z", "x"), 0, 0, tiled=True)
        oth = lax.ppermute(own, "core", [(0, 1), (1, 0)])
        buf = shape(PATCHES, KEYS, HEAD)
        att, *bufs = call(
            functools.partial(attend_kernel, turn, last),
            f"attend{turn}",
            [shape(CHIPS, N, HEAD)] + ([] if last else [buf, buf]),
            [info, own, oth] + ([] if first else [kbuf, vbuf]),
            20,
            [pltpu.VMEM((PER, KEYS, HEAD), BF16)] * 2,
        )
        back = lax.all_to_all(att, ("z", "x"), 0, 0, tiled=True)
        args = [info, back, w_out, x] + ([] if first else [recv]) + [modulation]
        (new,) = call(
            functools.partial(output_kernel, turn, last),
            f"output{turn}",
            [shape(PATCHES, PD, D) if last else shape(N, D)],
            args + (hidden if last else []),
            20,
        )
        hidden.append(new)
        if not last:
            kbuf, vbuf = bufs
            recv = lax.ppermute(new, "pipe", [(i, i + 1) for i in range(LAYERS - 1)])
    (kept,) = call(collect_kernel, "collect", [shape(PATCHES, PD, 2 * D)], [info] + fresh, 20)
    return (hidden[-1].reshape(1, PATCHES * PD, D), kept.reshape(1, PATCHES * PD, 2, D))


def solution(mesh):
    fine = Mesh(mesh.devices.reshape(4, 4, 4, 2), ("pipe", "z", "x", "core"))
    seq = ("z", "x", "core")
    in_specs = (
        P(seq, None),
        P("pipe", None, None),
        P("pipe", None, None),
        P("pipe", None, None),
        P("pipe", None, None),
        P("pipe", seq, None, None),
        P(seq, None),
        P(),
    )
    out_specs = (P("pipe", seq, None), P("pipe", seq, None, None))
    return jax.shard_map(
        on_device, mesh=fine, in_specs=in_specs, out_specs=out_specs, check_vma=False
    )
```

```python
import functools
import math

import jax
import jax.numpy as jnp
import numpy as np
from jax import lax
from jax.experimental import pallas as pl
from jax.experimental.pallas import tpu as pltpu
from jax.sharding import Mesh
from jax.sharding import PartitionSpec as P

GROUPS = 2
PATCHES = 4
HEAD = 128
HEADS = 12
CHIPS = 16
PD = 24
D = 1536
LAYERS = 4
PER = PATCHES // GROUPS
N = PER * PD
QUERIES = CHIPS * PD
KEYS = 2 * CHIPS * PD
ROWS = PER * 3 * PD
WIDE = 4 * HEAD
F32 = jnp.float32
BF16 = jnp.bfloat16


def lane_rows():
    lane = np.arange(HEAD)
    pair = lane // 2
    axis = np.where(pair < 8, 0, np.where(pair < 36, 1, 2))
    start = np.where(pair < 8, 0, np.where(pair < 36, 8, 36))
    width = np.where(pair < 8, 16.0, 56.0)
    freq = np.power(10000.0, -2.0 * (pair - start) / width)
    rows = [axis == 0, axis == 1, axis == 2, freq, lane % 2 == 0, lane % 2 == 1]
    return np.stack(rows + rows[:2]).astype(np.float32)


def rotary_tables(positions, lanes):
    picked = lax.dot_general(
        positions.astype(F32).astype(BF16),
        lanes[0:3].astype(BF16),
        (((0,), (0,)), ((), ())),
        preferred_element_type=F32,
    )
    angle = picked * lanes[3:4]
    cos, sin = jnp.cos(angle), jnp.sin(angle)
    return jnp.concatenate([cos, -sin * lanes[4:5], sin * lanes[5:6]], axis=1)


def hats(x, gain, tab):
    inv = lax.rsqrt(jnp.mean(x * x, axis=-1, keepdims=True) + 1e-6)
    x = x * inv * gain
    return (
        x * tab[:, :HEAD]
        + pltpu.roll(x, HEAD - 1, 1) * tab[:, HEAD : 2 * HEAD]
        + pltpu.roll(x, 1, 1) * tab[:, 2 * HEAD :]
    )


def stage(info_ref, turn):
    section = info_ref[0]
    g = jnp.clip(turn - section, 0, GROUPS - 1)
    ids = [info_ref[1 + g * PER + j] for j in range(PER)]
    return section, g, ids


def rows_of(info_ref, turn, x_ref, recv_ref):
    section, _, ids = stage(info_ref, turn)
    own = jnp.concatenate([x_ref[p].astype(F32) for p in ids], axis=0)
    if recv_ref is None:
        return own
    return jnp.where(section == 0, own, recv_ref[...].astype(F32))


def project_kernel(turn, *refs):
    first = turn == 0
    refs = list(refs)
    info_ref, x_ref = refs[:2]
    refs = refs[2:]
    recv_ref = None if first else refs.pop(0)
    mod_ref, w_ref, gain_ref = refs[:3]
    refs = refs[3:]
    q_gain = gain_ref[0, 0:1, :] * (math.log2(math.e) / math.sqrt(HEAD))
    k_gain = gain_ref[0, 1:2, :]
    if first:
        pos_ref, lane_ref, stale_ref, chunk_ref, fresh_ref, tab_ref, held_ref, sems = refs
        copies = []
        for block in range(D // WIDE):
            for part in range(3):
                cols = pl.ds(part * D + block * WIDE, WIDE)
                copies.append(
                    pltpu.make_async_copy(
                        w_ref.at[0, :, cols], held_ref.at[:, cols], sems.at[len(copies)]
                    )
                )
        for copy in copies[:6]:
            copy.start()
        tab_ref[...] = rotary_tables(pos_ref[...], lane_ref[...]).reshape(PATCHES, PD, 3 * HEAD)
        tabs = jnp.concatenate([tab_ref[info_ref[1 + r]] for r in range(1, PATCHES)], axis=0)

        def stale_block(block):
            ready = []
            for h in range(block * (WIDE // HEAD), (block + 1) * (WIDE // HEAD)):
                parts = []
                for r in range(1, PATCHES):
                    p = info_ref[1 + r]
                    ks = stale_ref[p, :, h * HEAD : (h + 1) * HEAD].astype(F32)
                    vs = stale_ref[p, :, D + h * HEAD : D + (h + 1) * HEAD].astype(F32)
                    parts += [ks, vs]
                ready.append((h, parts))
            for i, (h, parts) in enumerate(ready):
                ks = jnp.concatenate(parts[0::2], axis=0)
                ks = hats(ks, k_gain, tabs)
                for r in range(3):
                    parts[2 * r] = ks[PD * r : PD * (r + 1)]
                ready[i] = (h, jnp.concatenate(parts, axis=0).astype(BF16))
            for h, rows in ready:
                chunk_ref[h, ROWS:] = rows

    else:
        tab_ref, chunk_ref, fresh_ref = refs
    _, _, ids = stage(info_ref, turn)
    rows = rows_of(info_ref, turn, x_ref, recv_ref)
    centred = rows - jnp.mean(rows, axis=-1, keepdims=True)
    spread = jnp.mean(centred * centred, axis=-1, keepdims=True)
    modulated = (
        centred * lax.rsqrt(spread + 1e-6) * (1.0 + mod_ref[1]) + mod_ref[0]
    ).astype(BF16)
    tab = jnp.concatenate([tab_ref[p] for p in ids], axis=0)
    for c in range(HEADS, CHIPS):
        chunk_ref[c] = jnp.zeros(chunk_ref.shape[1:], BF16)
    for block in range(D // WIDE):
        if first and block == 0:
            stale_block(0)
            for copy in copies[6:]:
                copy.start()
        done = []
        for part in range(3):
            cols = slice(part * D + block * WIDE, part * D + (block + 1) * WIDE)
            if first:
                copies[3 * block + part].wait()
                w = held_ref[:, cols]
            else:
                w = w_ref[0, :, cols]
            done.append(jnp.dot(modulated, w, preferred_element_type=F32))
        if first and block + 1 < D // WIDE:
            stale_block(block + 1)
        q, k, v = done
        k16, v16 = k.astype(BF16), v.astype(BF16)
        fresh_ref[:, block * WIDE : (block + 1) * WIDE] = k16
        fresh_ref[:, D + block * WIDE : D + (block + 1) * WIDE] = v16
        k, v = k16.astype(F32), v16.astype(F32)
        for i in range(WIDE // HEAD):
            h = block * (WIDE // HEAD) + i
            lanes = slice(i * HEAD, (i + 1) * HEAD)
            qh = hats(q[:, lanes], q_gain, tab)
            kh = hats(k[:, lanes], k_gain, tab)
            vh = v[:, lanes]
            parts = []
            for j in range(PER):
                here = slice(PD * j, PD * (j + 1))
                parts += [qh[here], kh[here], vh[here]]
            chunk_ref[h, :ROWS] = jnp.concatenate(parts, axis=0).astype(BF16)


def taken(ref, start):
    rows = ref[...].astype(F32)[:, start : start + PD, :]
    return rows.reshape(CHIPS * PD, HEAD).astype(BF16)


def weighed(q, k, v):
    s = lax.dot_general(q, k, (((1,), (1,)), ((), ())), preferred_element_type=F32)
    w = jnp.exp2(s).astype(BF16)
    v = jnp.concatenate([v, jnp.ones(v.shape, BF16)], axis=1)
    return jnp.dot(w, v, preferred_element_type=F32)


def half(ref, q):
    k = [taken(ref, 3 * PD * j + PD) for j in range(PER)]
    v = [taken(ref, 3 * PD * j + 2 * PD) for j in range(PER)]
    return weighed(q, k[0], v[0]), weighed(q[QUERIES:], k[1], v[1])


def half_stale(ref, q):
    keys = [taken(ref, ROWS + 2 * PD * n) for n in range(3)]
    values = [taken(ref, ROWS + 2 * PD * n + PD) for n in range(3)]
    return sum(weighed(q, keys[n], values[n]) for n in (1, 2)), weighed(
        q[:QUERIES], keys[0], values[0]
    )


def both_queries(own_ref):
    return jnp.concatenate([taken(own_ref, 3 * PD * j) for j in range(PER)], axis=0)


def early_kernel(turn, info_ref, own_ref, *refs):
    first = turn == 0
    sum_ref = refs[-1]
    q = both_queries(own_ref)
    total, second = half(own_ref, q)
    if first:
        more, lead = half_stale(own_ref, q)
        total = total + more
    else:
        k_ref, v_ref = refs[:2]
        _, g, _ = stage(info_ref, turn)
        base = g * PER
        lead = weighed(q[:QUERIES], k_ref[base + 1], v_ref[base + 1])
        for n in range(PATCHES - PER):
            slot = jnp.where(n < base, n, n + PER)
            total = total + weighed(q, k_ref[slot], v_ref[slot])
    sum_ref[:QUERIES] = total[:QUERIES] + lead
    sum_ref[QUERIES:] = total[QUERIES:] + second


def late_kernel(turn, own_ref, oth_ref, sum_ref, out_ref):
    q = both_queries(own_ref)
    total, second = half(oth_ref, q)
    total = total + sum_ref[...]
    lead, second = total[:QUERIES], total[QUERIES:] + second
    if turn == 0:
        more, extra = half_stale(oth_ref, q)
        lead = lead + more[:QUERIES] + extra
        second = second + more[QUERIES:]
    outs = [
        (t[:, :HEAD] / t[:, HEAD:]).reshape(CHIPS, PD, HEAD) for t in (lead, second)
    ]
    out_ref[...] = jnp.concatenate(outs, axis=1).astype(BF16)


def keep_kernel(turn, info_ref, raw_ref, own_ref, oth_ref, *refs):
    section, g, _ = stage(info_ref, turn)
    kout_ref, vout_ref, pair_ref = refs[-3:]
    paired(raw_ref, pair_ref)
    pairs = ((own_ref, 0), (oth_ref, CHIPS * PD))

    def put(slot, start, old_ref, new_ref, keep):
        for ref, row in pairs:
            fresh = taken(ref, start)
            if old_ref is not None:
                old = old_ref[slot, row : row + CHIPS * PD]
                fresh = jnp.where(keep, fresh, old)
            new_ref[slot, row : row + CHIPS * PD] = fresh

    if turn == 0:
        put(0, PD, None, kout_ref, None)
        put(0, 2 * PD, None, vout_ref, None)
        for r in range(1, PATCHES):
            put(r, ROWS + 2 * PD * (r - 1), None, kout_ref, None)
            put(r, ROWS + 2 * PD * (r - 1) + PD, None, vout_ref, None)
        for j in range(1, PER):
            put(j, 3 * PD * j + PD, kout_ref, kout_ref, section == 0)
            put(j, 3 * PD * j + 2 * PD, vout_ref, vout_ref, section == 0)
        return
    kin_ref, vin_ref = refs[:2]
    base = g * PER
    begun = turn >= section
    for n in range(PATCHES - PER):
        slot = jnp.where(n < base, n, n + PER)
        kout_ref[slot] = kin_ref[slot]
        vout_ref[slot] = vin_ref[slot]
    for j in range(PER):
        put(base + j, 3 * PD * j + PD, kin_ref, kout_ref, begun)
        put(base + j, 3 * PD * j + 2 * PD, vin_ref, vout_ref, begun)


def output_kernel(turn, last, *refs):
    first = turn == 0
    refs = list(refs)
    info_ref, att_ref, w_ref, x_ref = refs[:4]
    refs = refs[4:]
    recv_ref = None if first else refs.pop(0)
    mod_ref = refs.pop(0)
    att = jnp.concatenate([att_ref[h] for h in range(HEADS)], axis=1)
    rows = rows_of(info_ref, turn, x_ref, recv_ref)
    branch = jnp.dot(att, w_ref[0], preferred_element_type=F32)
    new = rows + mod_ref[2] * branch
    if not last:
        refs[0][...] = new.astype(BF16)
        return
    *olds, out_ref = refs
    for section in range(LAYERS):

        @pl.when(info_ref[0] == section)
        def _():
            for g in range(GROUPS):
                rows = new if section + g == turn else olds[section + g][...].astype(F32)
                for j in range(PER):
                    p = info_ref[1 + g * PER + j]
                    out_ref[p] = rows[PD * j : PD * (j + 1)].astype(BF16)


def paired(ref, out_ref):
    for j in range(PER):
        for c in range(0, D, WIDE):
            k, v = (
                ref[:, at : at + WIDE].astype(F32)[PD * j : PD * (j + 1)] for at in (c, D + c)
            )
            out_ref[j, :, :, c : c + WIDE] = jnp.stack([k, v], axis=1).astype(BF16)


def collect_kernel(info_ref, *refs):
    *olds, raw_ref, out_ref, last_ref = refs
    olds = olds + [last_ref]

    @pl.when(info_ref[0] == LAYERS - 1)
    def _():
        paired(raw_ref, last_ref)

    for section in range(LAYERS):

        @pl.when(info_ref[0] == section)
        def _():
            for g in range(GROUPS):
                for j in range(PER):
                    out_ref[info_ref[1 + g * PER + j]] = olds[section + g][j]


SMEM = pl.BlockSpec(memory_space=pltpu.SMEM)
VMEM = pl.BlockSpec(memory_space=pltpu.VMEM)
HBM = pl.BlockSpec(memory_space=pltpu.HBM)


def shape(*dims, dtype=BF16):
    return jax.ShapeDtypeStruct(dims, dtype)


def call(kernel, name, out_shape, args, limit=20, specs=None, scratch=(), flops=10**9):
    return pl.pallas_call(
        kernel,
        out_shape=out_shape,
        in_specs=specs or [SMEM] + [VMEM] * (len(args) - 1),
        out_specs=[VMEM] * len(out_shape),
        scratch_shapes=list(scratch),
        compiler_params=pltpu.CompilerParams(vmem_limit_bytes=limit * 2**20),
        cost_estimate=pl.CostEstimate(flops=flops, bytes_accessed=2**20, transcendentals=0),
        name=name,
    )(*args)


def on_device(hidden_in, modulation, w_qkv, w_out, qk_gain, stale_kv, positions, order):
    section = lax.axis_index("pipe")
    info = jnp.concatenate([jnp.stack([section]).astype(jnp.int32), order])
    x = hidden_in.reshape(PATCHES, PD, D)
    modulation = jnp.transpose(modulation, (1, 0, 2))
    stale = stale_kv[0].reshape(PATCHES, PD, 2 * D)
    turns = GROUPS + LAYERS - 1
    recv = kbuf = vbuf = tab = None
    fresh, hidden = [], []
    buf = shape(PATCHES, KEYS, HEAD)
    for turn in range(turns):
        first, last = turn == 0, turn == turns - 1
        if first:
            chunk, raw, tab = call(
                functools.partial(project_kernel, turn),
                "project0",
                [
                    shape(CHIPS, ROWS + 3 * 2 * PD, HEAD),
                    shape(N, 2 * D),
                    shape(PATCHES, PD, 3 * HEAD, dtype=F32),
                ],
                [info, x, modulation, w_qkv, qk_gain, positions.T, jnp.asarray(lane_rows()), stale],
                40,
                [SMEM, VMEM, VMEM, HBM, VMEM, VMEM, VMEM, VMEM],
                [pltpu.VMEM((D, 3 * D), BF16), pltpu.SemaphoreType.DMA((9,))],
            )
        else:
            chunk, raw = call(
                functools.partial(project_kernel, turn),
                f"project{turn}",
                [shape(CHIPS, ROWS, HEAD), shape(N, 2 * D)],
                [info, x, recv, modulation, w_qkv, qk_gain, tab],
            )
        own = lax.all_to_all(chunk, ("z", "x"), 0, 0, tiled=True)
        oth = lax.ppermute(own, "core", [(0, 1), (1, 0)])
        (sums,) = call(
            functools.partial(early_kernel, turn),
            f"early{turn}",
            [shape(PER * QUERIES, 2 * HEAD, dtype=F32)],
            [info, own] + ([] if first else [kbuf, vbuf]),
            flops=3 * 10**9,
        )
        if last:
            (kept,) = call(
                collect_kernel,
                "collect",
                [shape(PATCHES, PD, 2, D)],
                [info] + fresh + [raw],
                scratch=[pltpu.VMEM((PER, PD, 2, D), BF16)],
            )
            kept = kept.reshape(1, PATCHES * PD, 2, D)
            oth, kept = lax.optimization_barrier((oth, kept))
        (att,) = call(
            functools.partial(late_kernel, turn),
            f"late{turn}",
            [shape(CHIPS, N, HEAD)],
            [own, oth, sums],
            specs=[VMEM] * 3,
        )
        back = lax.all_to_all(att, ("z", "x"), 0, 0, tiled=True)
        args = [info, back, w_out, x] + ([] if first else [recv]) + [modulation]
        (new,) = call(
            functools.partial(output_kernel, turn, last),
            f"output{turn}",
            [shape(PATCHES, PD, D) if last else shape(N, D)],
            args + (hidden if last else []),
        )
        hidden.append(new)
        if not last:
            kbuf, vbuf, pair = call(
                functools.partial(keep_kernel, turn),
                f"keep{turn}",
                [buf, buf, shape(PER, PD, 2, D)],
                [info, raw, own, oth] + ([] if first else [kbuf, vbuf]),
            )
            fresh.append(pair)
            recv = lax.ppermute(new, "pipe", [(i, i + 1) for i in range(LAYERS - 1)])
            recv, kbuf, vbuf = lax.optimization_barrier((recv, kbuf, vbuf))
    return (hidden[-1].reshape(1, PATCHES * PD, D), kept)


def solution(mesh):
    fine = Mesh(mesh.devices.reshape(4, 4, 4, 2), ("pipe", "z", "x", "core"))
    seq = ("z", "x", "core")
    in_specs = (
        P(seq, None),
        P("pipe", None, None),
        P("pipe", None, None),
        P("pipe", None, None),
        P("pipe", None, None),
        P("pipe", seq, None, None),
        P(seq, None),
        P(),
    )
    out_specs = (P("pipe", seq, None), P("pipe", seq, None, None))
    return jax.shard_map(
        on_device, mesh=fine, in_specs=in_specs, out_specs=out_specs, check_vma=False
    )
```

```python
import functools
import math

import jax
import jax.numpy as jnp
import numpy as np
from jax import lax
from jax.experimental import pallas as pl
from jax.experimental.pallas import tpu as pltpu
from jax.sharding import Mesh
from jax.sharding import PartitionSpec as P

GROUPS = 2
PATCHES = 4
HEAD = 128
HEADS = 12
CHIPS = 16
PD = 24
D = 1536
LAYERS = 4
PER = PATCHES // GROUPS
N = PER * PD
QUERIES = CHIPS * PD
KEYS = 2 * CHIPS * PD
ROWS = PER * 3 * PD
WIDE = 4 * HEAD
F32 = jnp.float32
BF16 = jnp.bfloat16


def lane_rows():
    lane = np.arange(HEAD)
    pair = lane // 2
    axis = np.where(pair < 8, 0, np.where(pair < 36, 1, 2))
    start = np.where(pair < 8, 0, np.where(pair < 36, 8, 36))
    width = np.where(pair < 8, 16.0, 56.0)
    freq = np.power(10000.0, -2.0 * (pair - start) / width)
    rows = [axis == 0, axis == 1, axis == 2, freq, lane % 2 == 0, lane % 2 == 1]
    return np.stack(rows + rows[:2]).astype(np.float32)


def rotary_tables(positions, lanes):
    picked = lax.dot_general(
        positions.astype(F32).astype(BF16),
        lanes[0:3].astype(BF16),
        (((0,), (0,)), ((), ())),
        preferred_element_type=F32,
    )
    angle = picked * lanes[3:4]
    cos, sin = jnp.cos(angle), jnp.sin(angle)
    return jnp.concatenate([cos, -sin * lanes[4:5], sin * lanes[5:6]], axis=1)


def hats(x, gain, tab, by_dot=False):
    if by_dot:
        ones = jnp.ones((HEAD, HEAD), BF16)
        square = x * x
        high = square.astype(BF16)
        low = (square - high.astype(F32)).astype(BF16)
        square = sum(jnp.dot(t, ones, preferred_element_type=F32) for t in (high, low)) / HEAD
    else:
        square = jnp.mean(x * x, axis=-1, keepdims=True)
    inv = lax.rsqrt(square + 1e-6)
    x = x * inv * gain
    return (
        x * tab[:, :HEAD]
        + pltpu.roll(x, HEAD - 1, 1) * tab[:, HEAD : 2 * HEAD]
        + pltpu.roll(x, 1, 1) * tab[:, 2 * HEAD :]
    )


def stage(info_ref, turn):
    section = info_ref[0]
    g = jnp.clip(turn - section, 0, GROUPS - 1)
    ids = [info_ref[1 + g * PER + j] for j in range(PER)]
    return section, g, ids


def rows_of(info_ref, turn, x_ref, recv_ref):
    section, _, ids = stage(info_ref, turn)
    own = jnp.concatenate([x_ref[p].astype(F32) for p in ids], axis=0)
    if recv_ref is None:
        return own
    sent = jnp.concatenate([recv_ref[j].astype(F32) for j in range(PER)], axis=0)
    return jnp.where(section == 0, own, sent)


def project_kernel(turn, last, *refs):
    first = turn == 0
    refs = list(refs)
    info_ref, x_ref = refs[:2]
    refs = refs[2:]
    recv_ref = None if first else refs.pop(0)
    mod_ref, w_ref, gain_ref = refs[:3]
    refs = refs[3:]
    q_gain = gain_ref[0, 0:1, :] * (math.log2(math.e) / math.sqrt(HEAD))
    k_gain = gain_ref[0, 1:2, :]
    if first:
        pos_ref, lane_ref, stale_ref, chunk_ref, fresh_ref, tab_ref, held_ref, sems = refs
        copies = []
        for block in range(D // WIDE):
            for part in range(3):
                cols = pl.ds(part * D + block * WIDE, WIDE)
                copies.append(
                    pltpu.make_async_copy(
                        w_ref.at[0, :, cols], held_ref.at[:, cols], sems.at[len(copies)]
                    )
                )
        for copy in copies[:6]:
            copy.start()
        tab_ref[...] = rotary_tables(pos_ref[...], lane_ref[...]).reshape(PATCHES, PD, 3 * HEAD)
        tabs = jnp.concatenate([tab_ref[info_ref[1 + r]] for r in range(1, PATCHES)], axis=0)

        def stale_block(block):
            ready = []
            for h in range(block * (WIDE // HEAD), (block + 1) * (WIDE // HEAD)):
                parts = []
                for r in range(1, PATCHES):
                    p = info_ref[1 + r]
                    ks = stale_ref[p, :, h * HEAD : (h + 1) * HEAD].astype(F32)
                    vs = stale_ref[p, :, D + h * HEAD : D + (h + 1) * HEAD].astype(F32)
                    parts += [ks, vs]
                ready.append((h, parts))
            for i, (h, parts) in enumerate(ready):
                ks = jnp.concatenate(parts[0::2], axis=0)
                ks = hats(ks, k_gain, tabs, by_dot=True)
                for r in range(3):
                    parts[2 * r] = ks[PD * r : PD * (r + 1)]
                ready[i] = (h, jnp.concatenate(parts, axis=0).astype(BF16))
            for h, rows in ready:
                chunk_ref[h, ROWS:] = rows

    else:
        tab_ref, chunk_ref, fresh_ref = refs
    _, _, ids = stage(info_ref, turn)
    rows = rows_of(info_ref, turn, x_ref, recv_ref)
    centred = rows - jnp.mean(rows, axis=-1, keepdims=True)
    spread = jnp.mean(centred * centred, axis=-1, keepdims=True)
    modulated = (
        centred * lax.rsqrt(spread + 1e-6) * (1.0 + mod_ref[1]) + mod_ref[0]
    ).astype(BF16)
    tab = jnp.concatenate([tab_ref[p] for p in ids], axis=0)
    for c in range(HEADS, CHIPS):
        chunk_ref[c] = jnp.zeros(chunk_ref.shape[1:], BF16)
    for block in range(D // WIDE):
        if first and block == 0:
            stale_block(0)
            for copy in copies[6:]:
                copy.start()
        done = []
        for part in range(3):
            cols = slice(part * D + block * WIDE, part * D + (block + 1) * WIDE)
            if first:
                copies[3 * block + part].wait()
                w = held_ref[:, cols]
            else:
                w = w_ref[0, :, cols]
            done.append(jnp.dot(modulated, w, preferred_element_type=F32))
        if first and block + 1 < D // WIDE:
            stale_block(block + 1)
        q, k, v = done
        k16, v16 = k.astype(BF16), v.astype(BF16)
        k, v = k16.astype(F32), v16.astype(F32)
        here = slice(block * WIDE, (block + 1) * WIDE)
        if last:
            for j in range(PER):
                both = [t[PD * j : PD * (j + 1)] for t in (k, v)]
                fresh_ref[j, :, :, here] = jnp.stack(both, axis=1).astype(BF16)
        else:
            fresh_ref[:, here] = k16
            fresh_ref[:, D + block * WIDE : D + (block + 1) * WIDE] = v16
        for i in range(WIDE // HEAD):
            h = block * (WIDE // HEAD) + i
            lanes = slice(i * HEAD, (i + 1) * HEAD)
            qh = hats(q[:, lanes], q_gain, tab)
            kh = hats(k[:, lanes], k_gain, tab)
            vh = v[:, lanes]
            parts = []
            for j in range(PER):
                here = slice(PD * j, PD * (j + 1))
                parts += [qh[here], kh[here], vh[here]]
            chunk_ref[h, :ROWS] = jnp.concatenate(parts, axis=0).astype(BF16)


def taken(ref, start):
    rows = ref[...].astype(F32)[:, start : start + PD, :]
    return rows.reshape(CHIPS * PD, HEAD).astype(BF16)


def weighed(q, k, v):
    s = lax.dot_general(q, k, (((1,), (1,)), ((), ())), preferred_element_type=F32)
    w = jnp.exp2(s).astype(BF16)
    v = jnp.concatenate([v, jnp.ones(v.shape, BF16)], axis=1)
    return jnp.dot(w, v, preferred_element_type=F32)


def half(ref, q):
    k = [taken(ref, 3 * PD * j + PD) for j in range(PER)]
    v = [taken(ref, 3 * PD * j + 2 * PD) for j in range(PER)]
    return weighed(q, k[0], v[0]), weighed(q[QUERIES:], k[1], v[1])


def half_stale(ref, q):
    keys = [taken(ref, ROWS + 2 * PD * n) for n in range(3)]
    values = [taken(ref, ROWS + 2 * PD * n + PD) for n in range(3)]
    return sum(weighed(q, keys[n], values[n]) for n in (1, 2)), weighed(
        q[:QUERIES], keys[0], values[0]
    )


def both_queries(own_ref):
    return jnp.concatenate([taken(own_ref, 3 * PD * j) for j in range(PER)], axis=0)


def early_kernel(turn, info_ref, own_ref, *refs):
    first = turn == 0
    sum_ref = refs[-1]
    q = both_queries(own_ref)
    total, second = half(own_ref, q)
    if first:
        more, lead = half_stale(own_ref, q)
        total = total + more
    else:
        k_ref, v_ref = refs[:2]
        _, g, _ = stage(info_ref, turn)
        base = g * PER
        lead = weighed(q[:QUERIES], k_ref[base + 1], v_ref[base + 1])
        for n in range(PATCHES - PER):
            slot = jnp.where(n < base, n, n + PER)
            total = total + weighed(q, k_ref[slot], v_ref[slot])
    sum_ref[:QUERIES] = total[:QUERIES] + lead
    sum_ref[QUERIES:] = total[QUERIES:] + second


def late_kernel(turn, own_ref, oth_ref, sum_ref, out_ref):
    q = both_queries(own_ref)
    total, second = half(oth_ref, q)
    total = total + sum_ref[...]
    lead, second = total[:QUERIES], total[QUERIES:] + second
    if turn == 0:
        more, extra = half_stale(oth_ref, q)
        lead = lead + more[:QUERIES] + extra
        second = second + more[QUERIES:]
    outs = [
        (t[:, :HEAD] / t[:, HEAD:]).reshape(CHIPS, PD, HEAD) for t in (lead, second)
    ]
    out_ref[...] = jnp.concatenate(outs, axis=1).astype(BF16)


def keep_kernel(turn, info_ref, raw_ref, own_ref, oth_ref, *refs):
    section, g, _ = stage(info_ref, turn)
    kout_ref, vout_ref, pair_ref = refs[-3:]
    paired(raw_ref, pair_ref)
    pairs = ((own_ref, 0), (oth_ref, CHIPS * PD))

    def put(slot, start, old_ref, new_ref, keep):
        for ref, row in pairs:
            fresh = taken(ref, start)
            if old_ref is not None:
                old = old_ref[slot, row : row + CHIPS * PD]
                fresh = jnp.where(keep, fresh, old)
            new_ref[slot, row : row + CHIPS * PD] = fresh

    if turn == 0:
        put(0, PD, None, kout_ref, None)
        put(0, 2 * PD, None, vout_ref, None)
        for r in range(1, PATCHES):
            put(r, ROWS + 2 * PD * (r - 1), None, kout_ref, None)
            put(r, ROWS + 2 * PD * (r - 1) + PD, None, vout_ref, None)
        for j in range(1, PER):
            put(j, 3 * PD * j + PD, kout_ref, kout_ref, section == 0)
            put(j, 3 * PD * j + 2 * PD, vout_ref, vout_ref, section == 0)
        return
    kin_ref, vin_ref = refs[:2]
    base = g * PER
    begun = turn >= section
    for n in range(PATCHES - PER):
        slot = jnp.where(n < base, n, n + PER)
        kout_ref[slot] = kin_ref[slot]
        vout_ref[slot] = vin_ref[slot]
    for j in range(PER):
        put(base + j, 3 * PD * j + PD, kin_ref, kout_ref, begun)
        put(base + j, 3 * PD * j + 2 * PD, vin_ref, vout_ref, begun)


def paired(ref, out_ref):
    for j in range(PER):
        for c in range(0, D, WIDE):
            k, v = (
                ref[:, at : at + WIDE].astype(F32)[PD * j : PD * (j + 1)] for at in (c, D + c)
            )
            out_ref[j, :, :, c : c + WIDE] = jnp.stack([k, v], axis=1).astype(BF16)


def place(info_ref, section, olds, out_ref, sems, skip=None):
    copies = []
    for g in range(GROUPS):
        if section + g == skip:
            continue
        for j in range(PER):
            r = g * PER + j
            copies.append(
                pltpu.make_async_copy(
                    olds[section + g].at[j], out_ref.at[info_ref[1 + r]], sems.at[r]
                )
            )
            copies[-1].start()
    return copies


def output_kernel(turn, last, *refs):
    first = turn == 0
    refs = list(refs)
    info_ref, att_ref, w_ref, x_ref = refs[:4]
    refs = refs[4:]
    recv_ref = None if first else refs.pop(0)
    mod_ref = refs.pop(0)

    def store(ref):
        att = jnp.concatenate([att_ref[h] for h in range(HEADS)], axis=1)
        rows = rows_of(info_ref, turn, x_ref, recv_ref)
        branch = jnp.dot(att, w_ref[0], preferred_element_type=F32)
        new = rows + mod_ref[2] * branch
        for j in range(PER):
            ref[j] = new[PD * j : PD * (j + 1)].astype(BF16)

    if not last:
        store(refs[0])
        return
    *refs, out_ref, kept_ref, new_ref, sems, kept_sems = refs
    fresh = refs[: turn + 1]
    olds = refs[turn + 1 :] + [new_ref]
    for section in range(LAYERS):

        @pl.when(info_ref[0] == section)
        def _():
            copies = place(info_ref, section, fresh, kept_ref, kept_sems)
            copies += place(info_ref, section, olds, out_ref, sems, turn)
            if section == LAYERS - 1:
                store(new_ref)
                copies += place(info_ref, section, olds, out_ref, sems, turn - 1)
            for copy in copies:
                copy.wait()


SMEM = pl.BlockSpec(memory_space=pltpu.SMEM)
VMEM = pl.BlockSpec(memory_space=pltpu.VMEM)
HBM = pl.BlockSpec(memory_space=pltpu.HBM)


def shape(*dims, dtype=BF16):
    return jax.ShapeDtypeStruct(dims, dtype)


def call(
    kernel, name, out_shape, args, limit=20, specs=None, scratch=(), flops=10**9, outs=None
):
    return pl.pallas_call(
        kernel,
        out_shape=out_shape,
        in_specs=specs or [SMEM] + [VMEM] * (len(args) - 1),
        out_specs=[outs or VMEM] * len(out_shape),
        scratch_shapes=list(scratch),
        compiler_params=pltpu.CompilerParams(vmem_limit_bytes=limit * 2**20),
        cost_estimate=pl.CostEstimate(flops=flops, bytes_accessed=2**20, transcendentals=0),
        name=name,
    )(*args)


def on_device(hidden_in, modulation, w_qkv, w_out, qk_gain, stale_kv, positions, order):
    section = lax.axis_index("pipe")
    info = jnp.concatenate([jnp.stack([section]).astype(jnp.int32), order])
    x = hidden_in.reshape(PATCHES, PD, D)
    modulation = jnp.transpose(modulation, (1, 0, 2))
    stale = stale_kv[0].reshape(PATCHES, PD, 2 * D)
    turns = GROUPS + LAYERS - 1
    recv = kbuf = vbuf = tab = None
    fresh, hidden = [], []
    buf = shape(PATCHES, KEYS, HEAD)
    for turn in range(turns):
        first, last = turn == 0, turn == turns - 1
        if first:
            chunk, raw, tab = call(
                functools.partial(project_kernel, turn, last),
                "project0",
                [
                    shape(CHIPS, ROWS + 3 * 2 * PD, HEAD),
                    shape(N, 2 * D),
                    shape(PATCHES, PD, 3 * HEAD, dtype=F32),
                ],
                [info, x, modulation, w_qkv, qk_gain, positions.T, jnp.asarray(lane_rows()), stale],
                40,
                [SMEM, VMEM, VMEM, HBM, VMEM, VMEM, VMEM, VMEM],
                [pltpu.VMEM((D, 3 * D), BF16), pltpu.SemaphoreType.DMA((9,))],
            )
        else:
            chunk, raw = call(
                functools.partial(project_kernel, turn, last),
                f"project{turn}",
                [
                    shape(CHIPS, ROWS, HEAD),
                    shape(PER, PD, 2, D) if last else shape(N, 2 * D),
                ],
                [info, x, recv, modulation, w_qkv, qk_gain, tab],
            )
        own = lax.all_to_all(chunk, ("z", "x"), 0, 0, tiled=True)
        oth = lax.ppermute(own, "core", [(0, 1), (1, 0)])
        (sums,) = call(
            functools.partial(early_kernel, turn),
            f"early{turn}",
            [shape(PER * QUERIES, 2 * HEAD, dtype=F32)],
            [info, own] + ([] if first else [kbuf, vbuf]),
            flops=3 * 10**9,
        )
        (att,) = call(
            functools.partial(late_kernel, turn),
            f"late{turn}",
            [shape(CHIPS, N, HEAD)],
            [own, oth, sums],
            specs=[VMEM] * 3,
        )
        back = lax.all_to_all(att, ("z", "x"), 0, 0, tiled=True)
        args = [info, back, w_out, x] + ([] if first else [recv]) + [modulation]
        new, *kept = call(
            functools.partial(output_kernel, turn, last),
            f"output{turn}",
            [shape(PATCHES, PD, D), shape(PATCHES, PD, 2, D)] if last else [shape(PER, PD, D)],
            args + (fresh + [raw] + hidden if last else []),
            scratch=[pltpu.VMEM((PER, PD, D), BF16)] + [pltpu.SemaphoreType.DMA((PATCHES,))] * 2
            if last
            else (),
            outs=HBM if last else None,
        )
        hidden.append(new)
        if not last:
            kbuf, vbuf, pair = call(
                functools.partial(keep_kernel, turn),
                f"keep{turn}",
                [buf, buf, shape(PER, PD, 2, D)],
                [info, raw, own, oth] + ([] if first else [kbuf, vbuf]),
            )
            fresh.append(pair)
            recv = lax.ppermute(new, "pipe", [(i, i + 1) for i in range(LAYERS - 1)])
            recv, kbuf, vbuf = lax.optimization_barrier((recv, kbuf, vbuf))
    return (
        hidden[-1].reshape(1, PATCHES * PD, D),
        kept[0].reshape(1, PATCHES * PD, 2, D),
    )


def solution(mesh):
    fine = Mesh(mesh.devices.reshape(4, 4, 4, 2), ("pipe", "z", "x", "core"))
    seq = ("z", "x", "core")
    in_specs = (
        P(seq, None),
        P("pipe", None, None),
        P("pipe", None, None),
        P("pipe", None, None),
        P("pipe", None, None),
        P("pipe", seq, None, None),
        P(seq, None),
        P(),
    )
    out_specs = (P("pipe", seq, None), P("pipe", seq, None, None))
    return jax.shard_map(
        on_device, mesh=fine, in_specs=in_specs, out_specs=out_specs, check_vma=False
    )
```

```python
import functools
import math

import jax
import jax.numpy as jnp
from jax import lax
from jax.experimental import pallas as pl
from jax.experimental.pallas import tpu as pltpu
from jax.sharding import Mesh
from jax.sharding import PartitionSpec as P

GROUPS = 2
PATCHES = 4
HEAD = 128
HEADS = 12
CHIPS = 16
PD = 24
D = 1536
LAYERS = 4
PER = PATCHES // GROUPS
N = PER * PD
QUERIES = CHIPS * PD
KEYS = 2 * CHIPS * PD
ROWS = PER * 3 * PD
WIDE = 4 * HEAD
F32 = jnp.float32
BF16 = jnp.bfloat16


def rotary_tables(positions):
    lane = lax.broadcasted_iota(jnp.int32, (8, HEAD), 1)
    row = lax.broadcasted_iota(jnp.int32, (8, HEAD), 0)
    pair = lane >> 1
    axis = jnp.where(pair < 8, 0, jnp.where(pair < 36, 1, 2))
    start = jnp.where(pair < 8, 0, jnp.where(pair < 36, 8, 36))
    width = jnp.where(pair < 8, 16.0, 56.0)
    freq = jnp.exp((pair - start).astype(F32) / width * (-2.0 * math.log(10000.0)))[0:1]
    even = jnp.where((lane & 1) == 0, 1.0, 0.0)[0:1]
    picks = jnp.where(axis == row, 1.0, 0.0)[0:3].astype(BF16)
    angle = freq * lax.dot_general(
        positions.astype(F32).astype(BF16),
        picks,
        (((0,), (0,)), ((), ())),
        preferred_element_type=F32,
    )
    cos, sin = jnp.cos(angle), jnp.sin(angle)
    return jnp.concatenate([cos, -sin * even, sin * (1.0 - even)], axis=1)


def hats(x, gain, tab, by_dot=False):
    if by_dot:
        ones = jnp.ones((HEAD, HEAD), BF16)
        square = x * x
        high = square.astype(BF16)
        low = (square - high.astype(F32)).astype(BF16)
        square = sum(jnp.dot(t, ones, preferred_element_type=F32) for t in (high, low)) / HEAD
    else:
        square = jnp.mean(x * x, axis=-1, keepdims=True)
    inv = lax.rsqrt(square + 1e-6)
    x = x * inv * gain
    return (
        x * tab[:, :HEAD]
        + pltpu.roll(x, HEAD - 1, 1) * tab[:, HEAD : 2 * HEAD]
        + pltpu.roll(x, 1, 1) * tab[:, 2 * HEAD :]
    )


def stage(info_ref, turn):
    section = info_ref[0]
    g = jnp.clip(turn - section, 0, GROUPS - 1)
    ids = [info_ref[1 + g * PER + j] for j in range(PER)]
    return section, g, ids


def rows_of(info_ref, turn, x_ref, recv_ref):
    section, _, ids = stage(info_ref, turn)
    own = jnp.concatenate([x_ref[p].astype(F32) for p in ids], axis=0)
    if recv_ref is None:
        return own
    sent = jnp.concatenate([recv_ref[j].astype(F32) for j in range(PER)], axis=0)
    return jnp.where(section == 0, own, sent)


def lanes_from(start):
    if isinstance(start, int):
        return slice(start, start + WIDE)
    return pl.ds(pl.multiple_of(start, WIDE), WIDE)


def project_kernel(turn, last, *refs):
    first = turn == 0
    refs = list(refs)
    info_ref, x_ref = refs[:2]
    refs = refs[2:]
    recv_ref = None if first else refs.pop(0)
    mod_ref, w_ref, gain_ref = refs[:3]
    refs = refs[3:]
    q_gain = gain_ref[0, 0:1, :] * (math.log2(math.e) / math.sqrt(HEAD))
    k_gain = gain_ref[0, 1:2, :]
    if first:
        pos_ref, stale_ref, chunk_ref, fresh_ref, tab_ref, held_ref, sems = refs
        copies = []
        for block in range(D // WIDE):
            for part in range(3):
                cols = pl.ds(part * D + block * WIDE, WIDE)
                copies.append(
                    pltpu.make_async_copy(
                        w_ref.at[0, :, cols], held_ref.at[:, cols], sems.at[len(copies)]
                    )
                )
        for copy in copies[:6]:
            copy.start()
        tab_ref[...] = rotary_tables(pos_ref[...]).reshape(PATCHES, PD, 3 * HEAD)
        tabs = jnp.concatenate([tab_ref[info_ref[1 + r]] for r in range(1, PATCHES)], axis=0)

        def stale_block(block):
            ready = []
            for h in range(block * (WIDE // HEAD), (block + 1) * (WIDE // HEAD)):
                parts = []
                for r in range(1, PATCHES):
                    p = info_ref[1 + r]
                    ks = stale_ref[p, :, h * HEAD : (h + 1) * HEAD].astype(F32)
                    vs = stale_ref[p, :, D + h * HEAD : D + (h + 1) * HEAD].astype(F32)
                    parts += [ks, vs]
                ready.append((h, parts))
            for i, (h, parts) in enumerate(ready):
                ks = jnp.concatenate(parts[0::2], axis=0)
                ks = hats(ks, k_gain, tabs, by_dot=True)
                for r in range(3):
                    parts[2 * r] = ks[PD * r : PD * (r + 1)]
                ready[i] = (h, jnp.concatenate(parts, axis=0).astype(BF16))
            for h, rows in ready:
                chunk_ref[h, ROWS:] = rows

    else:
        tab_ref, chunk_ref, fresh_ref = refs
    _, _, ids = stage(info_ref, turn)
    rows = rows_of(info_ref, turn, x_ref, recv_ref)
    centred = rows - jnp.mean(rows, axis=-1, keepdims=True)
    spread = jnp.mean(centred * centred, axis=-1, keepdims=True)
    modulated = (
        centred * lax.rsqrt(spread + 1e-6) * (1.0 + mod_ref[1]) + mod_ref[0]
    ).astype(BF16)
    tab = jnp.concatenate([tab_ref[p] for p in ids], axis=0)
    for c in range(HEADS, CHIPS):
        chunk_ref[c] = jnp.zeros(chunk_ref.shape[1:], BF16)
    def step(block, carry):
        if first and block == 0:
            stale_block(0)
            for copy in copies[6:]:
                copy.start()
        done = []
        for part in range(3):
            cols = lanes_from(part * D + block * WIDE)
            if first:
                copies[3 * block + part].wait()
                w = held_ref[:, cols]
            else:
                w = w_ref[0, :, cols]
            done.append(jnp.dot(modulated, w, preferred_element_type=F32))
        if first and block + 1 < D // WIDE:
            stale_block(block + 1)
        q, k, v = done
        k16, v16 = k.astype(BF16), v.astype(BF16)
        k, v = k16.astype(F32), v16.astype(F32)
        here = lanes_from(block * WIDE)
        if last:
            for j in range(PER):
                both = [t[PD * j : PD * (j + 1)] for t in (k, v)]
                fresh_ref[j, :, :, here] = jnp.stack(both, axis=1).astype(BF16)
        else:
            fresh_ref[:, here] = k16
            fresh_ref[:, lanes_from(D + block * WIDE)] = v16
        for i in range(WIDE // HEAD):
            h = block * (WIDE // HEAD) + i
            lanes = slice(i * HEAD, (i + 1) * HEAD)
            qh = hats(q[:, lanes], q_gain, tab)
            kh = hats(k[:, lanes], k_gain, tab)
            vh = v[:, lanes]
            parts = []
            for j in range(PER):
                here = slice(PD * j, PD * (j + 1))
                parts += [qh[here], kh[here], vh[here]]
            chunk_ref[h, :ROWS] = jnp.concatenate(parts, axis=0).astype(BF16)
        return carry

    if first:
        for block in range(D // WIDE):
            step(block, 0)
    else:
        lax.fori_loop(0, D // WIDE, step, 0)


def taken(ref, start):
    rows = ref[...].astype(F32)[:, start : start + PD, :]
    return rows.reshape(CHIPS * PD, HEAD).astype(BF16)


def weighed(q, k, v):
    s = lax.dot_general(q, k, (((1,), (1,)), ((), ())), preferred_element_type=F32)
    w = jnp.exp2(s).astype(BF16)
    v = jnp.concatenate([v, jnp.ones(v.shape, BF16)], axis=1)
    return jnp.dot(w, v, preferred_element_type=F32)


def half(ref, q):
    k = [taken(ref, 3 * PD * j + PD) for j in range(PER)]
    v = [taken(ref, 3 * PD * j + 2 * PD) for j in range(PER)]
    return weighed(q, k[0], v[0]), weighed(q[QUERIES:], k[1], v[1])


def half_stale(ref, q):
    keys = [taken(ref, ROWS + 2 * PD * n) for n in range(3)]
    values = [taken(ref, ROWS + 2 * PD * n + PD) for n in range(3)]
    return sum(weighed(q, keys[n], values[n]) for n in (1, 2)), weighed(
        q[:QUERIES], keys[0], values[0]
    )


def both_queries(own_ref):
    return jnp.concatenate([taken(own_ref, 3 * PD * j) for j in range(PER)], axis=0)


def early_kernel(turn, info_ref, own_ref, *refs):
    first = turn == 0
    sum_ref = refs[-1]
    q = both_queries(own_ref)
    total, second = half(own_ref, q)
    if first:
        more, lead = half_stale(own_ref, q)
        total = total + more
    else:
        k_ref, v_ref = refs[:2]
        _, g, _ = stage(info_ref, turn)
        base = g * PER
        lead = weighed(q[:QUERIES], k_ref[base + 1], v_ref[base + 1])
        for n in range(PATCHES - PER):
            slot = jnp.where(n < base, n, n + PER)
            total = total + weighed(q, k_ref[slot], v_ref[slot])
    sum_ref[:QUERIES] = total[:QUERIES] + lead
    sum_ref[QUERIES:] = total[QUERIES:] + second


def late_kernel(turn, own_ref, oth_ref, sum_ref, out_ref):
    q = both_queries(own_ref)
    total, second = half(oth_ref, q)
    total = total + sum_ref[...]
    lead, second = total[:QUERIES], total[QUERIES:] + second
    if turn == 0:
        more, extra = half_stale(oth_ref, q)
        lead = lead + more[:QUERIES] + extra
        second = second + more[QUERIES:]
    outs = [
        (t[:, :HEAD] / t[:, HEAD:]).reshape(CHIPS, PD, HEAD) for t in (lead, second)
    ]
    out_ref[...] = jnp.concatenate(outs, axis=1).astype(BF16)


def keep_kernel(turn, info_ref, raw_ref, own_ref, oth_ref, *refs):
    section, g, _ = stage(info_ref, turn)
    kout_ref, vout_ref, pair_ref = refs[-3:]
    paired(raw_ref, pair_ref)
    pairs = ((own_ref, 0), (oth_ref, CHIPS * PD))

    def put(slot, start, old_ref, new_ref, keep):
        for ref, row in pairs:
            fresh = taken(ref, start)
            if old_ref is not None:
                old = old_ref[slot, row : row + CHIPS * PD]
                fresh = jnp.where(keep, fresh, old)
            new_ref[slot, row : row + CHIPS * PD] = fresh

    if turn == 0:
        put(0, PD, None, kout_ref, None)
        put(0, 2 * PD, None, vout_ref, None)
        for r in range(1, PATCHES):
            put(r, ROWS + 2 * PD * (r - 1), None, kout_ref, None)
            put(r, ROWS + 2 * PD * (r - 1) + PD, None, vout_ref, None)
        for j in range(1, PER):
            put(j, 3 * PD * j + PD, kout_ref, kout_ref, section == 0)
            put(j, 3 * PD * j + 2 * PD, vout_ref, vout_ref, section == 0)
        return
    kin_ref, vin_ref = refs[:2]
    base = g * PER
    begun = turn >= section
    for n in range(PATCHES - PER):
        slot = jnp.where(n < base, n, n + PER)
        kout_ref[slot] = kin_ref[slot]
        vout_ref[slot] = vin_ref[slot]
    for j in range(PER):
        put(base + j, 3 * PD * j + PD, kin_ref, kout_ref, begun)
        put(base + j, 3 * PD * j + 2 * PD, vin_ref, vout_ref, begun)


def paired(ref, out_ref):
    for j in range(PER):
        for c in range(0, D, WIDE):
            k, v = (
                ref[:, at : at + WIDE].astype(F32)[PD * j : PD * (j + 1)] for at in (c, D + c)
            )
            out_ref[j, :, :, c : c + WIDE] = jnp.stack([k, v], axis=1).astype(BF16)


def place(info_ref, section, olds, out_ref, sems, skip=None):
    copies = []
    for g in range(GROUPS):
        if section + g == skip:
            continue
        for j in range(PER):
            r = g * PER + j
            copies.append(
                pltpu.make_async_copy(
                    olds[section + g].at[j], out_ref.at[info_ref[1 + r]], sems.at[r]
                )
            )
            copies[-1].start()
    return copies


def output_kernel(turn, last, *refs):
    first = turn == 0
    refs = list(refs)
    info_ref, att_ref, w_ref, x_ref = refs[:4]
    refs = refs[4:]
    recv_ref = None if first else refs.pop(0)
    mod_ref = refs.pop(0)

    def store(ref):
        att = jnp.concatenate([att_ref[h] for h in range(HEADS)], axis=1)
        rows = rows_of(info_ref, turn, x_ref, recv_ref)
        branch = jnp.dot(att, w_ref[0], preferred_element_type=F32)
        new = rows + mod_ref[2] * branch
        for j in range(PER):
            ref[j] = new[PD * j : PD * (j + 1)].astype(BF16)

    if not last:
        store(refs[0])
        return
    *refs, out_ref, kept_ref, new_ref, sems, kept_sems = refs
    fresh = refs[: turn + 1]
    olds = refs[turn + 1 :] + [new_ref]
    for section in range(LAYERS):

        @pl.when(info_ref[0] == section)
        def _():
            copies = place(info_ref, section, fresh, kept_ref, kept_sems)
            copies += place(info_ref, section, olds, out_ref, sems, turn)
            if section == LAYERS - 1:
                store(new_ref)
                copies += place(info_ref, section, olds, out_ref, sems, turn - 1)
            for copy in copies:
                copy.wait()


SMEM = pl.BlockSpec(memory_space=pltpu.SMEM)
VMEM = pl.BlockSpec(memory_space=pltpu.VMEM)
HBM = pl.BlockSpec(memory_space=pltpu.HBM)


def shape(*dims, dtype=BF16):
    return jax.ShapeDtypeStruct(dims, dtype)


def call(
    kernel, name, out_shape, args, limit=20, specs=None, scratch=(), flops=10**9, outs=None
):
    return pl.pallas_call(
        kernel,
        out_shape=out_shape,
        in_specs=specs or [SMEM] + [VMEM] * (len(args) - 1),
        out_specs=[outs or VMEM] * len(out_shape),
        scratch_shapes=list(scratch),
        compiler_params=pltpu.CompilerParams(vmem_limit_bytes=limit * 2**20),
        cost_estimate=pl.CostEstimate(flops=flops, bytes_accessed=2**20, transcendentals=0),
        name=name,
    )(*args)


def on_device(hidden_in, modulation, w_qkv, w_out, qk_gain, stale_kv, positions, order):
    section = lax.axis_index("pipe")
    info = jnp.concatenate([jnp.stack([section]).astype(jnp.int32), order])
    x = hidden_in.reshape(PATCHES, PD, D)
    modulation = jnp.transpose(modulation, (1, 0, 2))
    stale = stale_kv[0].reshape(PATCHES, PD, 2 * D)
    turns = GROUPS + LAYERS - 1
    recv = kbuf = vbuf = tab = None
    fresh, hidden = [], []
    buf = shape(PATCHES, KEYS, HEAD)
    for turn in range(turns):
        first, last = turn == 0, turn == turns - 1
        if first:
            chunk, raw, tab = call(
                functools.partial(project_kernel, turn, last),
                "project0",
                [
                    shape(CHIPS, ROWS + 3 * 2 * PD, HEAD),
                    shape(N, 2 * D),
                    shape(PATCHES, PD, 3 * HEAD, dtype=F32),
                ],
                [info, x, modulation, w_qkv, qk_gain, positions.T, stale],
                40,
                [SMEM, VMEM, VMEM, HBM, VMEM, VMEM, VMEM],
                [pltpu.VMEM((D, 3 * D), BF16), pltpu.SemaphoreType.DMA((9,))],
            )
        else:
            chunk, raw = call(
                functools.partial(project_kernel, turn, last),
                f"project{turn}",
                [
                    shape(CHIPS, ROWS, HEAD),
                    shape(PER, PD, 2, D) if last else shape(N, 2 * D),
                ],
                [info, x, recv, modulation, w_qkv, qk_gain, tab],
            )
        own = lax.all_to_all(chunk, ("z", "x"), 0, 0, tiled=True)
        oth = lax.ppermute(own, "core", [(0, 1), (1, 0)])
        (sums,) = call(
            functools.partial(early_kernel, turn),
            f"early{turn}",
            [shape(PER * QUERIES, 2 * HEAD, dtype=F32)],
            [info, own] + ([] if first else [kbuf, vbuf]),
            flops=3 * 10**9,
        )
        (att,) = call(
            functools.partial(late_kernel, turn),
            f"late{turn}",
            [shape(CHIPS, N, HEAD)],
            [own, oth, sums],
            specs=[VMEM] * 3,
        )
        back = lax.all_to_all(att, ("z", "x"), 0, 0, tiled=True)
        args = [info, back, w_out, x] + ([] if first else [recv]) + [modulation]
        new, *kept = call(
            functools.partial(output_kernel, turn, last),
            f"output{turn}",
            [shape(PATCHES, PD, D), shape(PATCHES, PD, 2, D)] if last else [shape(PER, PD, D)],
            args + (fresh + [raw] + hidden if last else []),
            scratch=[pltpu.VMEM((PER, PD, D), BF16)] + [pltpu.SemaphoreType.DMA((PATCHES,))] * 2
            if last
            else (),
            outs=HBM if last else None,
        )
        hidden.append(new)
        if not last:
            kbuf, vbuf, pair = call(
                functools.partial(keep_kernel, turn),
                f"keep{turn}",
                [buf, buf, shape(PER, PD, 2, D)],
                [info, raw, own, oth] + ([] if first else [kbuf, vbuf]),
            )
            fresh.append(pair)
            recv = lax.ppermute(new, "pipe", [(i, i + 1) for i in range(LAYERS - 1)])
            recv, kbuf, vbuf = lax.optimization_barrier((recv, kbuf, vbuf))
    return (
        hidden[-1].reshape(1, PATCHES * PD, D),
        kept[0].reshape(1, PATCHES * PD, 2, D),
    )


def solution(mesh):
    fine = Mesh(mesh.devices.reshape(4, 4, 4, 2), ("pipe", "z", "x", "core"))
    seq = ("z", "x", "core")
    in_specs = (
        P(seq, None),
        P("pipe", None, None),
        P("pipe", None, None),
        P("pipe", None, None),
        P("pipe", None, None),
        P("pipe", seq, None, None),
        P(seq, None),
        P(),
    )
    out_specs = (P("pipe", seq, None), P("pipe", seq, None, None))
    return jax.shard_map(
        on_device, mesh=fine, in_specs=in_specs, out_specs=out_specs, check_vma=False
    )
```

```python
import functools
import math

import jax
import jax.numpy as jnp
from jax import lax
from jax.experimental import pallas as pl
from jax.experimental.pallas import tpu as pltpu
from jax.sharding import Mesh
from jax.sharding import PartitionSpec as P

GROUPS = 2
PATCHES = 4
HEAD = 128
HEADS = 12
CHIPS = 16
PD = 24
D = 1536
LAYERS = 4
PER = PATCHES // GROUPS
N = PER * PD
QUERIES = CHIPS * PD
KEYS = 2 * CHIPS * PD
ROWS = PER * 3 * PD
WIDE = 4 * HEAD
F32 = jnp.float32
BF16 = jnp.bfloat16


def rotary_tables(positions):
    lane = lax.broadcasted_iota(jnp.int32, (8, HEAD), 1)
    row = lax.broadcasted_iota(jnp.int32, (8, HEAD), 0)
    pair = lane >> 1
    axis = jnp.where(pair < 8, 0, jnp.where(pair < 36, 1, 2))
    start = jnp.where(pair < 8, 0, jnp.where(pair < 36, 8, 36))
    width = jnp.where(pair < 8, 16.0, 56.0)
    freq = jnp.exp((pair - start).astype(F32) / width * (-2.0 * math.log(10000.0)))[0:1]
    even = jnp.where((lane & 1) == 0, 1.0, 0.0)[0:1]
    picks = jnp.where(axis == row, 1.0, 0.0)[0:3].astype(BF16)
    angle = freq * lax.dot_general(
        positions.astype(F32).astype(BF16),
        picks,
        (((0,), (0,)), ((), ())),
        preferred_element_type=F32,
    )
    cos, sin = jnp.cos(angle), jnp.sin(angle)
    return jnp.concatenate([cos, -sin * even, sin * (1.0 - even)], axis=1)


def hats(x, gain, tab, by_dot=False):
    if by_dot:
        ones = jnp.ones((HEAD, HEAD), BF16)
        square = x * x
        high = square.astype(BF16)
        low = (square - high.astype(F32)).astype(BF16)
        square = sum(jnp.dot(t, ones, preferred_element_type=F32) for t in (high, low)) / HEAD
    else:
        square = jnp.mean(x * x, axis=-1, keepdims=True)
    inv = lax.rsqrt(square + 1e-6)
    x = x * inv * gain
    return (
        x * tab[:, :HEAD]
        + pltpu.roll(x, HEAD - 1, 1) * tab[:, HEAD : 2 * HEAD]
        + pltpu.roll(x, 1, 1) * tab[:, 2 * HEAD :]
    )


def stage(info_ref, turn):
    section = info_ref[0]
    g = jnp.clip(turn - section, 0, GROUPS - 1)
    ids = [info_ref[1 + g * PER + j] for j in range(PER)]
    return section, g, ids


def rows_of(info_ref, turn, x_ref, recv_ref):
    section, _, ids = stage(info_ref, turn)
    own = jnp.concatenate([x_ref[p].astype(F32) for p in ids], axis=0)
    if recv_ref is None:
        return own
    sent = jnp.concatenate([recv_ref[j].astype(F32) for j in range(PER)], axis=0)
    return jnp.where(section == 0, own, sent)


def lanes_from(start):
    if isinstance(start, int):
        return slice(start, start + WIDE)
    return pl.ds(pl.multiple_of(start, WIDE), WIDE)


def project_kernel(turn, last, *refs):
    first = turn == 0
    refs = list(refs)
    info_ref, x_ref = refs[:2]
    refs = refs[2:]
    recv_ref = None if first else refs.pop(0)
    mod_ref, w_ref, gain_ref = refs[:3]
    refs = refs[3:]
    q_gain = gain_ref[0, 0:1, :] * (math.log2(math.e) / math.sqrt(HEAD))
    k_gain = gain_ref[0, 1:2, :]
    if first:
        pos_ref, stale_ref, chunk_ref, fresh_ref, tab_ref, held_ref, sems = refs
        copies = []
        for block in range(D // WIDE):
            for part in range(3):
                cols = pl.ds(part * D + block * WIDE, WIDE)
                copies.append(
                    pltpu.make_async_copy(
                        w_ref.at[0, :, cols], held_ref.at[:, cols], sems.at[len(copies)]
                    )
                )
        for copy in copies:
            copy.start()
        tab_ref[...] = rotary_tables(pos_ref[...]).reshape(PATCHES, PD, 3 * HEAD)
        tabs = jnp.concatenate([tab_ref[info_ref[1 + r]] for r in range(1, PATCHES)], axis=0)

        def stale_block(block):
            ready = []
            for h in range(block * (WIDE // HEAD), (block + 1) * (WIDE // HEAD)):
                parts = []
                for r in range(1, PATCHES):
                    p = info_ref[1 + r]
                    ks = stale_ref[p, :, h * HEAD : (h + 1) * HEAD].astype(F32)
                    vs = stale_ref[p, :, D + h * HEAD : D + (h + 1) * HEAD].astype(F32)
                    parts += [ks, vs]
                ready.append((h, parts))
            for i, (h, parts) in enumerate(ready):
                ks = jnp.concatenate(parts[0::2], axis=0)
                ks = hats(ks, k_gain, tabs, by_dot=True)
                for r in range(3):
                    parts[2 * r] = ks[PD * r : PD * (r + 1)]
                ready[i] = (h, jnp.concatenate(parts, axis=0).astype(BF16))
            for h, rows in ready:
                chunk_ref[h, ROWS:] = rows

    else:
        tab_ref, chunk_ref, fresh_ref = refs
    _, _, ids = stage(info_ref, turn)
    rows = rows_of(info_ref, turn, x_ref, recv_ref)
    centred = rows - jnp.mean(rows, axis=-1, keepdims=True)
    spread = jnp.mean(centred * centred, axis=-1, keepdims=True)
    modulated = (
        centred * lax.rsqrt(spread + 1e-6) * (1.0 + mod_ref[1]) + mod_ref[0]
    ).astype(BF16)
    tab = jnp.concatenate([tab_ref[p] for p in ids], axis=0)
    for c in range(HEADS, CHIPS):
        chunk_ref[c] = jnp.zeros(chunk_ref.shape[1:], BF16)
    def step(block, carry):
        if first and block == 0:
            stale_block(0)
        done = []
        for part in range(3):
            cols = lanes_from(part * D + block * WIDE)
            if first:
                copies[3 * block + part].wait()
                w = held_ref[:, cols]
            else:
                w = w_ref[0, :, cols]
            done.append(jnp.dot(modulated, w, preferred_element_type=F32))
        if first and block + 1 < D // WIDE:
            stale_block(block + 1)
        q, k, v = done
        k16, v16 = k.astype(BF16), v.astype(BF16)
        k, v = k16.astype(F32), v16.astype(F32)
        here = lanes_from(block * WIDE)
        if last:
            for j in range(PER):
                both = [t[PD * j : PD * (j + 1)] for t in (k, v)]
                fresh_ref[j, :, :, here] = jnp.stack(both, axis=1).astype(BF16)
        else:
            fresh_ref[:, here] = k16
            fresh_ref[:, lanes_from(D + block * WIDE)] = v16
        for i in range(WIDE // HEAD):
            h = block * (WIDE // HEAD) + i
            lanes = slice(i * HEAD, (i + 1) * HEAD)
            qh = hats(q[:, lanes], q_gain, tab)
            kh = hats(k[:, lanes], k_gain, tab)
            vh = v[:, lanes]
            parts = []
            for j in range(PER):
                here = slice(PD * j, PD * (j + 1))
                parts += [qh[here], kh[here], vh[here]]
            chunk_ref[h, :ROWS] = jnp.concatenate(parts, axis=0).astype(BF16)
        return carry

    if turn < 2:
        for block in range(D // WIDE):
            step(block, 0)
    else:
        lax.fori_loop(0, D // WIDE, step, 0)


def taken(ref, start):
    rows = ref[...].astype(F32)[:, start : start + PD, :]
    return rows.reshape(CHIPS * PD, HEAD).astype(BF16)


def weighed(q, k, v):
    s = lax.dot_general(q, k, (((1,), (1,)), ((), ())), preferred_element_type=F32)
    w = jnp.exp2(s).astype(BF16)
    v = jnp.concatenate([v, jnp.ones(v.shape, BF16)], axis=1)
    return jnp.dot(w, v, preferred_element_type=F32)


def half(ref, q):
    k = [taken(ref, 3 * PD * j + PD) for j in range(PER)]
    v = [taken(ref, 3 * PD * j + 2 * PD) for j in range(PER)]
    return weighed(q, k[0], v[0]), weighed(q[QUERIES:], k[1], v[1])


def half_stale(ref, q):
    keys = [taken(ref, ROWS + 2 * PD * n) for n in range(3)]
    values = [taken(ref, ROWS + 2 * PD * n + PD) for n in range(3)]
    return sum(weighed(q, keys[n], values[n]) for n in (1, 2)), weighed(
        q[:QUERIES], keys[0], values[0]
    )


def both_queries(own_ref):
    return jnp.concatenate([taken(own_ref, 3 * PD * j) for j in range(PER)], axis=0)


def early_kernel(turn, info_ref, own_ref, *refs):
    first = turn == 0
    sum_ref = refs[-1]
    q = both_queries(own_ref)
    total, second = half(own_ref, q)
    if first:
        more, lead = half_stale(own_ref, q)
        total = total + more
    else:
        k_ref, v_ref = refs[:2]
        _, g, _ = stage(info_ref, turn)
        base = g * PER
        lead = weighed(q[:QUERIES], k_ref[base + 1], v_ref[base + 1])
        for n in range(PATCHES - PER):
            slot = jnp.where(n < base, n, n + PER)
            total = total + weighed(q, k_ref[slot], v_ref[slot])
    sum_ref[:QUERIES] = total[:QUERIES] + lead
    sum_ref[QUERIES:] = total[QUERIES:] + second


def late_kernel(turn, own_ref, oth_ref, sum_ref, out_ref):
    q = both_queries(own_ref)
    total, second = half(oth_ref, q)
    total = total + sum_ref[...]
    lead, second = total[:QUERIES], total[QUERIES:] + second
    if turn == 0:
        more, extra = half_stale(oth_ref, q)
        lead = lead + more[:QUERIES] + extra
        second = second + more[QUERIES:]
    outs = [
        (t[:, :HEAD] / t[:, HEAD:]).reshape(CHIPS, PD, HEAD) for t in (lead, second)
    ]
    out_ref[...] = jnp.concatenate(outs, axis=1).astype(BF16)


def keep_kernel(turn, info_ref, raw_ref, own_ref, oth_ref, *refs):
    section, g, _ = stage(info_ref, turn)
    kout_ref, vout_ref, pair_ref = refs[-3:]
    paired(raw_ref, pair_ref)
    pairs = ((own_ref, 0), (oth_ref, CHIPS * PD))

    def put(slot, start, old_ref, new_ref, keep):
        for ref, row in pairs:
            fresh = taken(ref, start)
            if old_ref is not None:
                old = old_ref[slot, row : row + CHIPS * PD]
                fresh = jnp.where(keep, fresh, old)
            new_ref[slot, row : row + CHIPS * PD] = fresh

    if turn == 0:
        put(0, PD, None, kout_ref, None)
        put(0, 2 * PD, None, vout_ref, None)
        for r in range(1, PATCHES):
            put(r, ROWS + 2 * PD * (r - 1), None, kout_ref, None)
            put(r, ROWS + 2 * PD * (r - 1) + PD, None, vout_ref, None)
        for j in range(1, PER):
            put(j, 3 * PD * j + PD, kout_ref, kout_ref, section == 0)
            put(j, 3 * PD * j + 2 * PD, vout_ref, vout_ref, section == 0)
        return
    kin_ref, vin_ref = refs[:2]
    base = g * PER
    begun = turn >= section
    for n in range(PATCHES - PER):
        slot = jnp.where(n < base, n, n + PER)
        kout_ref[slot] = kin_ref[slot]
        vout_ref[slot] = vin_ref[slot]
    for j in range(PER):
        put(base + j, 3 * PD * j + PD, kin_ref, kout_ref, begun)
        put(base + j, 3 * PD * j + 2 * PD, vin_ref, vout_ref, begun)


def paired(ref, out_ref):
    for j in range(PER):
        for c in range(0, D, WIDE):
            k, v = (
                ref[:, at : at + WIDE].astype(F32)[PD * j : PD * (j + 1)] for at in (c, D + c)
            )
            out_ref[j, :, :, c : c + WIDE] = jnp.stack([k, v], axis=1).astype(BF16)


def place(info_ref, section, olds, out_ref, sems, skip=None):
    copies = []
    for g in range(GROUPS):
        if section + g == skip:
            continue
        for j in range(PER):
            r = g * PER + j
            copies.append(
                pltpu.make_async_copy(
                    olds[section + g].at[j], out_ref.at[info_ref[1 + r]], sems.at[r]
                )
            )
            copies[-1].start()
    return copies


def output_kernel(turn, last, *refs):
    first = turn == 0
    refs = list(refs)
    info_ref, att_ref, w_ref, x_ref = refs[:4]
    refs = refs[4:]
    recv_ref = None if first else refs.pop(0)
    mod_ref = refs.pop(0)

    def store(ref):
        att = jnp.concatenate([att_ref[h] for h in range(HEADS)], axis=1)
        rows = rows_of(info_ref, turn, x_ref, recv_ref)
        branch = jnp.dot(att, w_ref[0], preferred_element_type=F32)
        new = rows + mod_ref[2] * branch
        for j in range(PER):
            ref[j] = new[PD * j : PD * (j + 1)].astype(BF16)

    if not last:
        store(refs[0])
        return
    *refs, out_ref, kept_ref, new_ref, sems, kept_sems = refs
    fresh = refs[: turn + 1]
    olds = refs[turn + 1 :] + [new_ref]
    for section in range(LAYERS):

        @pl.when(info_ref[0] == section)
        def _():
            copies = place(info_ref, section, fresh, kept_ref, kept_sems)
            copies += place(info_ref, section, olds, out_ref, sems, turn)
            if section == LAYERS - 1:
                store(new_ref)
                copies += place(info_ref, section, olds, out_ref, sems, turn - 1)
            for copy in copies:
                copy.wait()


SMEM = pl.BlockSpec(memory_space=pltpu.SMEM)
VMEM = pl.BlockSpec(memory_space=pltpu.VMEM)
HBM = pl.BlockSpec(memory_space=pltpu.HBM)


def shape(*dims, dtype=BF16):
    return jax.ShapeDtypeStruct(dims, dtype)


def call(
    kernel, name, out_shape, args, limit=20, specs=None, scratch=(), flops=10**9, outs=None
):
    return pl.pallas_call(
        kernel,
        out_shape=out_shape,
        in_specs=specs or [SMEM] + [VMEM] * (len(args) - 1),
        out_specs=[outs or VMEM] * len(out_shape),
        scratch_shapes=list(scratch),
        compiler_params=pltpu.CompilerParams(vmem_limit_bytes=limit * 2**20),
        cost_estimate=pl.CostEstimate(flops=flops, bytes_accessed=2**20, transcendentals=0),
        name=name,
    )(*args)


def on_device(hidden_in, modulation, w_qkv, w_out, qk_gain, stale_kv, positions, order):
    section = lax.axis_index("pipe")
    info = jnp.concatenate([jnp.stack([section]).astype(jnp.int32), order])
    x = hidden_in.reshape(PATCHES, PD, D)
    modulation = jnp.transpose(modulation, (1, 0, 2))
    stale = stale_kv[0].reshape(PATCHES, PD, 2 * D)
    turns = GROUPS + LAYERS - 1
    recv = kbuf = vbuf = tab = None
    fresh, hidden = [], []
    buf = shape(PATCHES, KEYS, HEAD)
    for turn in range(turns):
        first, last = turn == 0, turn == turns - 1
        if first:
            chunk, raw, tab = call(
                functools.partial(project_kernel, turn, last),
                "project0",
                [
                    shape(CHIPS, ROWS + 3 * 2 * PD, HEAD),
                    shape(N, 2 * D),
                    shape(PATCHES, PD, 3 * HEAD, dtype=F32),
                ],
                [info, x, modulation, w_qkv, qk_gain, positions.T, stale],
                40,
                [SMEM, VMEM, VMEM, HBM, VMEM, VMEM, VMEM],
                [pltpu.VMEM((D, 3 * D), BF16), pltpu.SemaphoreType.DMA((9,))],
            )
        else:
            chunk, raw = call(
                functools.partial(project_kernel, turn, last),
                f"project{turn}",
                [
                    shape(CHIPS, ROWS, HEAD),
                    shape(PER, PD, 2, D) if last else shape(N, 2 * D),
                ],
                [info, x, recv, modulation, w_qkv, qk_gain, tab],
            )
        own = lax.all_to_all(chunk, ("z", "x"), 0, 0, tiled=True)
        oth = lax.ppermute(own, "core", [(0, 1), (1, 0)])
        (sums,) = call(
            functools.partial(early_kernel, turn),
            f"early{turn}",
            [shape(PER * QUERIES, 2 * HEAD, dtype=F32)],
            [info, own] + ([] if first else [kbuf, vbuf]),
            flops=3 * 10**9,
        )
        (att,) = call(
            functools.partial(late_kernel, turn),
            f"late{turn}",
            [shape(CHIPS, N, HEAD)],
            [own, oth, sums],
            specs=[VMEM] * 3,
        )
        back = lax.all_to_all(att, ("z", "x"), 0, 0, tiled=True)
        args = [info, back, w_out, x] + ([] if first else [recv]) + [modulation]
        new, *kept = call(
            functools.partial(output_kernel, turn, last),
            f"output{turn}",
            [shape(PATCHES, PD, D), shape(PATCHES, PD, 2, D)] if last else [shape(PER, PD, D)],
            args + (fresh + [raw] + hidden if last else []),
            scratch=[pltpu.VMEM((PER, PD, D), BF16)] + [pltpu.SemaphoreType.DMA((PATCHES,))] * 2
            if last
            else (),
            outs=HBM if last else None,
        )
        hidden.append(new)
        if not last:
            kbuf, vbuf, pair = call(
                functools.partial(keep_kernel, turn),
                f"keep{turn}",
                [buf, buf, shape(PER, PD, 2, D)],
                [info, raw, own, oth] + ([] if first else [kbuf, vbuf]),
            )
            fresh.append(pair)
            recv = lax.ppermute(new, "pipe", [(i, i + 1) for i in range(LAYERS - 1)])
            recv, kbuf, vbuf = lax.optimization_barrier((recv, kbuf, vbuf))
    return (
        hidden[-1].reshape(1, PATCHES * PD, D),
        kept[0].reshape(1, PATCHES * PD, 2, D),
    )


def solution(mesh):
    fine = Mesh(mesh.devices.reshape(4, 4, 4, 2), ("pipe", "z", "x", "core"))
    seq = ("z", "x", "core")
    in_specs = (
        P(seq, None),
        P("pipe", None, None),
        P("pipe", None, None),
        P("pipe", None, None),
        P("pipe", None, None),
        P("pipe", seq, None, None),
        P(seq, None),
        P(),
    )
    out_specs = (P("pipe", seq, None), P("pipe", seq, None, None))
    return jax.shard_map(
        on_device, mesh=fine, in_specs=in_specs, out_specs=out_specs, check_vma=False
    )
```

```python
import functools
import math

import jax
import jax.numpy as jnp
from jax import lax
from jax.experimental import pallas as pl
from jax.experimental.pallas import tpu as pltpu
from jax.sharding import Mesh
from jax.sharding import PartitionSpec as P

GROUPS = 2
PATCHES = 4
HEAD = 128
HEADS = 12
CHIPS = 16
PD = 24
D = 1536
LAYERS = 4
PER = PATCHES // GROUPS
N = PER * PD
QUERIES = CHIPS * PD
KEYS = 2 * CHIPS * PD
ROWS = PER * 3 * PD
WIDE = 4 * HEAD
F32 = jnp.float32
BF16 = jnp.bfloat16


def rotary_tables(positions):
    lane = lax.broadcasted_iota(jnp.int32, (8, HEAD), 1)
    row = lax.broadcasted_iota(jnp.int32, (8, HEAD), 0)
    pair = lane >> 1
    axis = jnp.where(pair < 8, 0, jnp.where(pair < 36, 1, 2))
    start = jnp.where(pair < 8, 0, jnp.where(pair < 36, 8, 36))
    width = jnp.where(pair < 8, 16.0, 56.0)
    freq = jnp.exp((pair - start).astype(F32) / width * (-2.0 * math.log(10000.0)))[0:1]
    even = jnp.where((lane & 1) == 0, 1.0, 0.0)[0:1]
    picks = jnp.where(axis == row, 1.0, 0.0)[0:3].astype(BF16)
    angle = freq * lax.dot_general(
        positions.astype(F32).astype(BF16),
        picks,
        (((0,), (0,)), ((), ())),
        preferred_element_type=F32,
    )
    cos, sin = jnp.cos(angle), jnp.sin(angle)
    return jnp.concatenate([cos, -sin * even, sin * (1.0 - even)], axis=1)


def hats(x, gain, tab, by_dot=False):
    if by_dot:
        ones = jnp.ones((HEAD, HEAD), BF16)
        square = x * x
        high = square.astype(BF16)
        low = (square - high.astype(F32)).astype(BF16)
        square = sum(jnp.dot(t, ones, preferred_element_type=F32) for t in (high, low)) / HEAD
    else:
        square = jnp.mean(x * x, axis=-1, keepdims=True)
    inv = lax.rsqrt(square + 1e-6)
    x = x * inv * gain
    return (
        x * tab[:, :HEAD]
        + pltpu.roll(x, HEAD - 1, 1) * tab[:, HEAD : 2 * HEAD]
        + pltpu.roll(x, 1, 1) * tab[:, 2 * HEAD :]
    )


def stage(info_ref, turn):
    section = info_ref[0]
    g = jnp.clip(turn - section, 0, GROUPS - 1)
    ids = [info_ref[1 + g * PER + j] for j in range(PER)]
    return section, g, ids


def rows_of(info_ref, turn, x_ref, recv_ref):
    section, _, ids = stage(info_ref, turn)
    own = jnp.concatenate([x_ref[p].astype(F32) for p in ids], axis=0)
    if recv_ref is None:
        return own
    sent = jnp.concatenate([recv_ref[j].astype(F32) for j in range(PER)], axis=0)
    return jnp.where(section == 0, own, sent)


def lanes_from(start):
    if isinstance(start, int):
        return slice(start, start + WIDE)
    return pl.ds(pl.multiple_of(start, WIDE), WIDE)


def project_kernel(turn, last, *refs):
    first = turn == 0
    refs = list(refs)
    info_ref, x_ref = refs[:2]
    refs = refs[2:]
    recv_ref = None if first else refs.pop(0)
    mod_ref, w_ref, gain_ref = refs[:3]
    refs = refs[3:]
    q_gain = gain_ref[0, 0:1, :] * (math.log2(math.e) / math.sqrt(HEAD))
    k_gain = gain_ref[0, 1:2, :]
    if first:
        pos_ref, stale_ref, chunk_ref, fresh_ref, tab_ref, held_ref, sems = refs
        copies = []
        for block in range(D // WIDE):
            for part in range(3):
                cols = pl.ds(part * D + block * WIDE, WIDE)
                copies.append(
                    pltpu.make_async_copy(
                        w_ref.at[0, :, cols], held_ref.at[:, cols], sems.at[len(copies)]
                    )
                )
        for copy in copies:
            copy.start()
        tab_ref[...] = rotary_tables(pos_ref[...]).reshape(PATCHES, PD, 3 * HEAD)
        tabs = jnp.concatenate([tab_ref[info_ref[1 + r]] for r in range(1, PATCHES)], axis=0)

        def stale_block(block):
            ready = []
            for h in range(block * (WIDE // HEAD), (block + 1) * (WIDE // HEAD)):
                parts = []
                for r in range(1, PATCHES):
                    p = info_ref[1 + r]
                    ks = stale_ref[p, :, h * HEAD : (h + 1) * HEAD].astype(F32)
                    vs = stale_ref[p, :, D + h * HEAD : D + (h + 1) * HEAD].astype(F32)
                    parts += [ks, vs]
                ready.append((h, parts))
            for i, (h, parts) in enumerate(ready):
                ks = jnp.concatenate(parts[0::2], axis=0)
                ks = hats(ks, k_gain, tabs, by_dot=True)
                for r in range(3):
                    parts[2 * r] = ks[PD * r : PD * (r + 1)]
                ready[i] = (h, jnp.concatenate(parts, axis=0).astype(BF16))
            for h, rows in ready:
                chunk_ref[h, ROWS:] = rows

    else:
        tab_ref, chunk_ref, fresh_ref = refs
    _, _, ids = stage(info_ref, turn)
    rows = rows_of(info_ref, turn, x_ref, recv_ref)
    centred = rows - jnp.mean(rows, axis=-1, keepdims=True)
    spread = jnp.mean(centred * centred, axis=-1, keepdims=True)
    modulated = (
        centred * lax.rsqrt(spread + 1e-6) * (1.0 + mod_ref[1]) + mod_ref[0]
    ).astype(BF16)
    tab = jnp.concatenate([tab_ref[p] for p in ids], axis=0)
    for c in range(HEADS, CHIPS):
        chunk_ref[c] = jnp.zeros(chunk_ref.shape[1:], BF16)
    def step(block, carry):
        if first and block == 0:
            stale_block(0)
        done = []
        for part in range(3):
            cols = lanes_from(part * D + block * WIDE)
            if first:
                copies[3 * block + part].wait()
                w = held_ref[:, cols]
            else:
                w = w_ref[0, :, cols]
            done.append(jnp.dot(modulated, w, preferred_element_type=F32))
        if first and block + 1 < D // WIDE:
            stale_block(block + 1)
        q, k, v = done
        k16, v16 = k.astype(BF16), v.astype(BF16)
        k, v = k16.astype(F32), v16.astype(F32)
        here = lanes_from(block * WIDE)
        if last:
            for j in range(PER):
                both = [t[PD * j : PD * (j + 1)] for t in (k, v)]
                fresh_ref[j, :, :, here] = jnp.stack(both, axis=1).astype(BF16)
        else:
            fresh_ref[:, here] = k16
            fresh_ref[:, lanes_from(D + block * WIDE)] = v16
        for i in range(WIDE // HEAD):
            h = block * (WIDE // HEAD) + i
            lanes = slice(i * HEAD, (i + 1) * HEAD)
            qh = hats(q[:, lanes], q_gain, tab)
            kh = hats(k[:, lanes], k_gain, tab)
            vh = v[:, lanes]
            parts = []
            for j in range(PER):
                here = slice(PD * j, PD * (j + 1))
                parts += [qh[here], kh[here], vh[here]]
            chunk_ref[h, :ROWS] = jnp.concatenate(parts, axis=0).astype(BF16)
        return carry

    if turn < 3:
        for block in range(D // WIDE):
            step(block, 0)
    else:
        lax.fori_loop(0, D // WIDE, step, 0)


def taken(ref, start):
    rows = ref[...].astype(F32)[:, start : start + PD, :]
    return rows.reshape(CHIPS * PD, HEAD).astype(BF16)


def weighed(q, k, v):
    s = lax.dot_general(q, k, (((1,), (1,)), ((), ())), preferred_element_type=F32)
    w = jnp.exp2(s).astype(BF16)
    v = jnp.concatenate([v, jnp.ones(v.shape, BF16)], axis=1)
    return jnp.dot(w, v, preferred_element_type=F32)


def half(ref, q):
    k = [taken(ref, 3 * PD * j + PD) for j in range(PER)]
    v = [taken(ref, 3 * PD * j + 2 * PD) for j in range(PER)]
    return weighed(q, k[0], v[0]), weighed(q[QUERIES:], k[1], v[1])


def half_stale(ref, q):
    keys = [taken(ref, ROWS + 2 * PD * n) for n in range(3)]
    values = [taken(ref, ROWS + 2 * PD * n + PD) for n in range(3)]
    return sum(weighed(q, keys[n], values[n]) for n in (1, 2)), weighed(
        q[:QUERIES], keys[0], values[0]
    )


def both_queries(own_ref):
    return jnp.concatenate([taken(own_ref, 3 * PD * j) for j in range(PER)], axis=0)


def early_kernel(turn, info_ref, own_ref, *refs):
    first = turn == 0
    sum_ref = refs[-1]
    q = both_queries(own_ref)
    total, second = half(own_ref, q)
    if first:
        more, lead = half_stale(own_ref, q)
        total = total + more
    else:
        k_ref, v_ref = refs[:2]
        _, g, _ = stage(info_ref, turn)
        base = g * PER
        lead = weighed(q[:QUERIES], k_ref[base + 1], v_ref[base + 1])
        for n in range(PATCHES - PER):
            slot = jnp.where(n < base, n, n + PER)
            total = total + weighed(q, k_ref[slot], v_ref[slot])
    sum_ref[:QUERIES] = total[:QUERIES] + lead
    sum_ref[QUERIES:] = total[QUERIES:] + second


def late_kernel(turn, own_ref, oth_ref, sum_ref, out_ref):
    q = both_queries(own_ref)
    total, second = half(oth_ref, q)
    total = total + sum_ref[...]
    lead, second = total[:QUERIES], total[QUERIES:] + second
    if turn == 0:
        more, extra = half_stale(oth_ref, q)
        lead = lead + more[:QUERIES] + extra
        second = second + more[QUERIES:]
    outs = [
        (t[:, :HEAD] / t[:, HEAD:]).reshape(CHIPS, PD, HEAD) for t in (lead, second)
    ]
    out_ref[...] = jnp.concatenate(outs, axis=1).astype(BF16)


def keep_kernel(turn, info_ref, raw_ref, own_ref, oth_ref, *refs):
    section, g, _ = stage(info_ref, turn)
    kout_ref, vout_ref, pair_ref = refs[-3:]
    paired(raw_ref, pair_ref)
    pairs = ((own_ref, 0), (oth_ref, CHIPS * PD))

    def put(slot, start, old_ref, new_ref, keep):
        for ref, row in pairs:
            fresh = taken(ref, start)
            if old_ref is not None:
                old = old_ref[slot, row : row + CHIPS * PD]
                fresh = jnp.where(keep, fresh, old)
            new_ref[slot, row : row + CHIPS * PD] = fresh

    if turn == 0:
        put(0, PD, None, kout_ref, None)
        put(0, 2 * PD, None, vout_ref, None)
        for r in range(1, PATCHES):
            put(r, ROWS + 2 * PD * (r - 1), None, kout_ref, None)
            put(r, ROWS + 2 * PD * (r - 1) + PD, None, vout_ref, None)
        for j in range(1, PER):
            put(j, 3 * PD * j + PD, kout_ref, kout_ref, section == 0)
            put(j, 3 * PD * j + 2 * PD, vout_ref, vout_ref, section == 0)
        return
    kin_ref, vin_ref = refs[:2]
    base = g * PER
    begun = turn >= section
    for n in range(PATCHES - PER):
        slot = jnp.where(n < base, n, n + PER)
        kout_ref[slot] = kin_ref[slot]
        vout_ref[slot] = vin_ref[slot]
    for j in range(PER):
        put(base + j, 3 * PD * j + PD, kin_ref, kout_ref, begun)
        put(base + j, 3 * PD * j + 2 * PD, vin_ref, vout_ref, begun)


def paired(ref, out_ref):
    for j in range(PER):
        for c in range(0, D, WIDE):
            k, v = (
                ref[:, at : at + WIDE].astype(F32)[PD * j : PD * (j + 1)] for at in (c, D + c)
            )
            out_ref[j, :, :, c : c + WIDE] = jnp.stack([k, v], axis=1).astype(BF16)


def place(info_ref, section, olds, out_ref, sems, skip=None):
    copies = []
    for g in range(GROUPS):
        if section + g == skip:
            continue
        for j in range(PER):
            r = g * PER + j
            copies.append(
                pltpu.make_async_copy(
                    olds[section + g].at[j], out_ref.at[info_ref[1 + r]], sems.at[r]
                )
            )
            copies[-1].start()
    return copies


def output_kernel(turn, last, *refs):
    first = turn == 0
    refs = list(refs)
    info_ref, att_ref, w_ref, x_ref = refs[:4]
    refs = refs[4:]
    recv_ref = None if first else refs.pop(0)
    mod_ref = refs.pop(0)

    def store(ref):
        att = jnp.concatenate([att_ref[h] for h in range(HEADS)], axis=1)
        rows = rows_of(info_ref, turn, x_ref, recv_ref)
        branch = jnp.dot(att, w_ref[0], preferred_element_type=F32)
        new = rows + mod_ref[2] * branch
        for j in range(PER):
            ref[j] = new[PD * j : PD * (j + 1)].astype(BF16)

    if not last:
        store(refs[0])
        return
    *refs, out_ref, kept_ref, new_ref, sems, kept_sems = refs
    fresh = refs[: turn + 1]
    olds = refs[turn + 1 :] + [new_ref]
    for section in range(LAYERS):

        @pl.when(info_ref[0] == section)
        def _():
            copies = place(info_ref, section, fresh, kept_ref, kept_sems)
            copies += place(info_ref, section, olds, out_ref, sems, turn)
            if section == LAYERS - 1:
                store(new_ref)
                copies += place(info_ref, section, olds, out_ref, sems, turn - 1)
            for copy in copies:
                copy.wait()


SMEM = pl.BlockSpec(memory_space=pltpu.SMEM)
VMEM = pl.BlockSpec(memory_space=pltpu.VMEM)
HBM = pl.BlockSpec(memory_space=pltpu.HBM)


def shape(*dims, dtype=BF16):
    return jax.ShapeDtypeStruct(dims, dtype)


def call(
    kernel, name, out_shape, args, limit=20, specs=None, scratch=(), flops=10**9, outs=None
):
    return pl.pallas_call(
        kernel,
        out_shape=out_shape,
        in_specs=specs or [SMEM] + [VMEM] * (len(args) - 1),
        out_specs=[outs or VMEM] * len(out_shape),
        scratch_shapes=list(scratch),
        compiler_params=pltpu.CompilerParams(vmem_limit_bytes=limit * 2**20),
        cost_estimate=pl.CostEstimate(flops=flops, bytes_accessed=2**20, transcendentals=0),
        name=name,
    )(*args)


def on_device(hidden_in, modulation, w_qkv, w_out, qk_gain, stale_kv, positions, order):
    section = lax.axis_index("pipe")
    info = jnp.concatenate([jnp.stack([section]).astype(jnp.int32), order])
    x = hidden_in.reshape(PATCHES, PD, D)
    modulation = jnp.transpose(modulation, (1, 0, 2))
    stale = stale_kv[0].reshape(PATCHES, PD, 2 * D)
    turns = GROUPS + LAYERS - 1
    recv = kbuf = vbuf = tab = None
    fresh, hidden = [], []
    buf = shape(PATCHES, KEYS, HEAD)
    for turn in range(turns):
        first, last = turn == 0, turn == turns - 1
        if first:
            chunk, raw, tab = call(
                functools.partial(project_kernel, turn, last),
                "project0",
                [
                    shape(CHIPS, ROWS + 3 * 2 * PD, HEAD),
                    shape(N, 2 * D),
                    shape(PATCHES, PD, 3 * HEAD, dtype=F32),
                ],
                [info, x, modulation, w_qkv, qk_gain, positions.T, stale],
                40,
                [SMEM, VMEM, VMEM, HBM, VMEM, VMEM, VMEM],
                [pltpu.VMEM((D, 3 * D), BF16), pltpu.SemaphoreType.DMA((9,))],
            )
        else:
            chunk, raw = call(
                functools.partial(project_kernel, turn, last),
                f"project{turn}",
                [
                    shape(CHIPS, ROWS, HEAD),
                    shape(PER, PD, 2, D) if last else shape(N, 2 * D),
                ],
                [info, x, recv, modulation, w_qkv, qk_gain, tab],
            )
        own = lax.all_to_all(chunk, ("z", "x"), 0, 0, tiled=True)
        oth = lax.ppermute(own, "core", [(0, 1), (1, 0)])
        (sums,) = call(
            functools.partial(early_kernel, turn),
            f"early{turn}",
            [shape(PER * QUERIES, 2 * HEAD, dtype=F32)],
            [info, own] + ([] if first else [kbuf, vbuf]),
            flops=3 * 10**9,
        )
        (att,) = call(
            functools.partial(late_kernel, turn),
            f"late{turn}",
            [shape(CHIPS, N, HEAD)],
            [own, oth, sums],
            specs=[VMEM] * 3,
        )
        back = lax.all_to_all(att, ("z", "x"), 0, 0, tiled=True)
        args = [info, back, w_out, x] + ([] if first else [recv]) + [modulation]
        new, *kept = call(
            functools.partial(output_kernel, turn, last),
            f"output{turn}",
            [shape(PATCHES, PD, D), shape(PATCHES, PD, 2, D)] if last else [shape(PER, PD, D)],
            args + (fresh + [raw] + hidden if last else []),
            scratch=[pltpu.VMEM((PER, PD, D), BF16)] + [pltpu.SemaphoreType.DMA((PATCHES,))] * 2
            if last
            else (),
            outs=HBM if last else None,
        )
        hidden.append(new)
        if not last:
            kbuf, vbuf, pair = call(
                functools.partial(keep_kernel, turn),
                f"keep{turn}",
                [buf, buf, shape(PER, PD, 2, D)],
                [info, raw, own, oth] + ([] if first else [kbuf, vbuf]),
            )
            fresh.append(pair)
            recv = lax.ppermute(new, "pipe", [(i, i + 1) for i in range(LAYERS - 1)])
            recv, kbuf, vbuf = lax.optimization_barrier((recv, kbuf, vbuf))
    return (
        hidden[-1].reshape(1, PATCHES * PD, D),
        kept[0].reshape(1, PATCHES * PD, 2, D),
    )


def solution(mesh):
    fine = Mesh(mesh.devices.reshape(4, 4, 4, 2), ("pipe", "z", "x", "core"))
    seq = ("z", "x", "core")
    in_specs = (
        P(seq, None),
        P("pipe", None, None),
        P("pipe", None, None),
        P("pipe", None, None),
        P("pipe", None, None),
        P("pipe", seq, None, None),
        P(seq, None),
        P(),
    )
    out_specs = (P("pipe", seq, None), P("pipe", seq, None, None))
    return jax.shard_map(
        on_device, mesh=fine, in_specs=in_specs, out_specs=out_specs, check_vma=False
    )
```
